128 devices in a mesh: grid: 32 (over y, x, core), lev: 4 (over z).
Axes of the slice: x: 4, y: 4, z: 4, core: 2. Of those that a mesh axis runs over, the one named last changes fastest.
Arguments:
- trajectory: float32 [32, 1280, 4096], P('lev', 'grid'), may hold values from -6 to 6
- legendre: float32 [640, 1280, 640], P(('grid', 'lev')), as said below
- obs_cell: int32 [65536], P('grid'), may hold values from 0 to 40959, as said below
- obs_count: int32 [1024], P('grid'), may hold values from 0 to 64, as said below
- departure: float32 [65536, 128], P('grid'), may hold values from -6 to 6
- obs_weight: float32 [32, 65536], P('lev', 'grid'), may hold values from -6 to 6
- band_of: int32 [32], replicated, may hold values from 0 to 31, each once
- m_order: int32 [640], replicated, may hold values from 0 to 639, as said below
Outputs:
- spectral: float32 [640, 32, 2, 640], P(('grid', 'lev'))
The draws below stay inside these ranges and needn't reach their ends.
Inputs may be any that keep to these rules, and one draw needn't show every extreme that they name: `obs_cell`: slots q * 64 to q * 64 + 63 of each device name blocks in rows q * 40 to q * 40 + 39. `obs_count`: some destination group receives 64 live slots from every device. `m_order`: each wavenumber once. legendre[j, l, n] is zero where n * 640 < m_order[j] * 640.
All inputs are finite; a program needn't handle non-finite values.
Results may differ from the reference program's by a relative error of at most 0.000098.
Values sent between devices are 32-bit elements; how exact they have to be, the bound alone decides.
No kernel may reach another device: no remote copies, remote signals or barrier semaphores. Data moves between devices by JAX's collectives and lax.ppermute only.
A program may use at most 128 MiB of HBM per device.

```python
import math
import jax
import jax.numpy as jnp
from jax import lax

CHAN = 32
NLAT = 1280
NLON = 4096
BLK = 128
M = 640
NN = 640
OBS_DEV = 2048
CAP = 64
NOBS = 65536
NBLK = 32
LAT_DEV = 40
N_GRID = 32


def order_draw(key):
    return jax.random.permutation(key, M).astype(jnp.int32)


def draw_m_order(key, part):
    return order_draw(key)


def draw_legendre(key, part):
    wavenumbers = order_draw(key)
    key = jax.random.fold_in(key, 2)
    values = jax.random.normal(key, (M, NLAT, NN), jnp.float32)
    total_index = jnp.arange(NN, dtype=jnp.int32)
    keep = (total_index[None, None, :] * M >= wavenumbers[:, None, None] * NN).astype(jnp.float32)
    return values * keep * (1.0 / math.sqrt(NLAT * NLON))


def draw_obs_cell(key, part):
    key = jax.random.fold_in(key, 3)
    rows_key, blocks_key = jax.random.split(key)
    slot_ids = jnp.arange(NOBS, dtype=jnp.int32)
    dest_group = slot_ids % OBS_DEV // CAP
    row_pick = dest_group * LAT_DEV + jax.random.randint(rows_key, (NOBS,), 0, LAT_DEV, dtype=jnp.int32)
    block_pick = jax.random.randint(blocks_key, (NOBS,), 0, NBLK, dtype=jnp.int32)
    cells = row_pick * NBLK + block_pick
    cells = cells.at[0].set(0)
    cells = cells.at[OBS_DEV - 1].set(NLAT * NBLK - 1)
    return cells.astype(jnp.int32)


def draw_obs_count(key, part):
    key = jax.random.fold_in(key, 4)
    keys = jax.random.split(key, 5)
    heavy = jax.random.randint(keys[0], (1, N_GRID), 0, 4, dtype=jnp.int32) == 0
    upper = jax.random.randint(keys[1], (N_GRID, N_GRID), CAP // 2, CAP + 1, dtype=jnp.int32)
    lower = jax.random.randint(keys[2], (N_GRID, N_GRID), 0, CAP // 2 + 1, dtype=jnp.int32)
    counts = jnp.where(heavy, upper, lower)
    full_group = jax.random.randint(keys[3], (), 0, N_GRID, dtype=jnp.int32)
    group_ids = jnp.arange(N_GRID, dtype=jnp.int32)
    counts = jnp.where(group_ids[None, :] == full_group, CAP, counts)
    picks = jax.random.randint(keys[4], (2,), 0, N_GRID, dtype=jnp.int32)
    empty_group = (full_group + 1 + picks[1] % (N_GRID - 1)) % N_GRID
    counts = counts.at[picks[0], empty_group].set(0)
    return counts.reshape(N_GRID * N_GRID).astype(jnp.int32)


def block_levels(key, shape, cuts, low, largest):
    loudness = 1.0
    for dim, blocks in cuts:
        heights = jax.random.uniform(jax.random.fold_in(jax.random.fold_in(key, 6), dim), (blocks,), jnp.float32, low / len(cuts), largest / len(cuts))
        loudness = loudness * jnp.repeat(jnp.exp(heights), shape[dim] // blocks).reshape((-1,) + (1,) * (len(shape) - 1 - dim))
    return loudness


def normal_values(stream_key, extent, spread, bound, cuts=(), kind=jnp.bfloat16):
    entries = jax.random.normal(stream_key, extent, jnp.float32) * spread
    if len(cuts) > 0:
        entries = block_levels(stream_key, extent, cuts, -0.22, 0.18) * entries
    return jnp.clip(entries, min=-bound, max=bound).astype(kind)


def setup_inputs(seed: int = 0) -> dict:
    seeds = jax.random.split(jax.random.key(seed), 9)
    trajectory = normal_values(seeds[0], (CHAN, NLAT, NLON), 1.0, 6.0, ((0, 4), (1, 32)), jnp.float32)
    legendre = draw_legendre(jax.random.fold_in(seeds[8], 71), 0)
    obs_cell = draw_obs_cell(jax.random.fold_in(seeds[8], 71), 0)
    obs_count = draw_obs_count(jax.random.fold_in(seeds[8], 71), 0)
    departure = normal_values(seeds[4], (NOBS, BLK), 1.0, 6.0, ((0, 32),), jnp.float32)
    obs_weight = normal_values(seeds[5], (CHAN, NOBS), 1.0, 6.0, ((0, 4), (1, 32)), jnp.float32)
    band_of = jax.random.permutation(seeds[6], N_GRID).astype(jnp.int32)
    m_order = draw_m_order(jax.random.fold_in(seeds[8], 71), 0)
    return {"trajectory": trajectory, "legendre": legendre, "obs_cell": obs_cell, "obs_count": obs_count, "departure": departure, "obs_weight": obs_weight, "band_of": band_of, "m_order": m_order}


def fourier_table(wavenumbers):
    lon_index = jnp.arange(NLON, dtype=jnp.int32)
    phase_index = (wavenumbers[:, None].astype(jnp.int32) * lon_index[None, :]) % NLON
    phase = (2.0 * math.pi / NLON) * phase_index.astype(jnp.float32)
    factor = jnp.where(wavenumbers == 0, 1.0, 2.0).astype(jnp.float32)[:, None]
    return jnp.stack([factor * jnp.cos(phase), -factor * jnp.sin(phase)], axis=1)


def reference(trajectory, legendre, obs_cell, obs_count, departure, obs_weight, band_of, m_order):
    slot_ids = jnp.arange(NOBS, dtype=jnp.int32)
    source = slot_ids // OBS_DEV
    dest_group = (slot_ids % OBS_DEV) // CAP
    live_mask = ((slot_ids % CAP) < obs_count[source * N_GRID + dest_group]).astype(jnp.float32)
    flat_traj = trajectory.reshape(CHAN, NLAT * NBLK, BLK)
    blocks = flat_traj[:, obs_cell, :]
    obs_grads = (obs_weight * live_mask[None, :])[:, :, None] * (1.0 + 0.5 * jnp.tanh(blocks)) * departure[None, :, :]
    adjoint_grid = jnp.zeros_like(flat_traj).at[:, obs_cell, :].add(obs_grads).reshape(CHAN, NLAT, NLON)
    trig_table = fourier_table(m_order)
    fourier = jnp.einsum("mpj,crj->mpcr", trig_table, adjoint_grid, precision=lax.Precision.HIGHEST)
    inverse = jnp.zeros((N_GRID,), jnp.int32).at[band_of].set(jnp.arange(N_GRID, dtype=jnp.int32))
    latitude = jnp.arange(NLAT, dtype=jnp.int32)
    row_of_lat = inverse[latitude // LAT_DEV] * LAT_DEV + latitude % LAT_DEV
    fourier_lat = fourier[:, :, :, row_of_lat]

    def one_slot(pair):
        coeffs, table_rows = pair
        return jnp.einsum("pcl,ln->cpn", coeffs, table_rows, precision=lax.Precision.HIGHEST)

    return lax.map(one_slot, (fourier_lat, legendre))
```

```python
import functools
import math

import jax
import jax.numpy as jnp
import numpy as np
from jax import lax
from jax.experimental import pallas as pl
from jax.experimental.pallas import tpu as pltpu
from jax.sharding import PartitionSpec as P

LANES = 128
SUB = 8
RADIX = 16
GROUPS = RADIX // 2
MIB = 1 << 20
F32 = jnp.float32
BF16 = jnp.bfloat16
I32 = jnp.int32


def wave_columns(wave_total):
    per_residue = wave_total // RADIX
    cols = np.full((GROUPS, LANES), -1, np.int32)
    for g in range(GROUPS):
        first, second = g, (RADIX - g if g else RADIX // 2)
        turns = RADIX * np.arange(per_residue)
        cols[g, :per_residue] = first + turns
        cols[g, per_residue : 2 * per_residue] = second + turns
    return cols


def wave_table(wave_total, lon_count):
    width = lon_count // RADIX
    cols = wave_columns(wave_total)
    per_residue = wave_total // RADIX
    fine = np.arange(width, dtype=np.int64)
    out = np.zeros((GROUPS, 2, width, 2, LANES), np.float64)
    for g in range(GROUPS):
        for i in range(2 * per_residue):
            m = int(cols[g, i])
            angle = 2.0 * math.pi / lon_count * ((m * fine) % lon_count)
            factor = 1.0 if m == 0 else 2.0
            cos, sin = factor * np.cos(angle), factor * np.sin(angle)
            second = i >= per_residue
            if g == 0:
                part = 1 if second else 0
                out[g, part, :, 0, i] = cos
                out[g, part, :, 1, i] = -sin
            else:
                sign = -1.0 if second else 1.0
                out[g, 0, :, 0, i] = cos
                out[g, 1, :, 0, i] = sign * sin
                out[g, 0, :, 1, i] = -sin
                out[g, 1, :, 1, i] = sign * cos
    return out.reshape(GROUPS, 2 * width, 2 * LANES).astype(np.float32)


def split_np(table):
    high = table.astype(jnp.bfloat16)
    low = (table - high.astype(np.float32)).astype(jnp.bfloat16)
    return high, low


def split(x):
    high = x.astype(BF16)
    return high, (x - high.astype(F32)).astype(BF16)


def real_fft(xs):
    n = len(xs)
    if n == 2:
        return [(xs[0] + xs[1], None), (xs[0] - xs[1], None)]
    even, odd = real_fft(xs[0::2]), real_fft(xs[1::2])
    out = [None] * (n // 2 + 1)
    for k in range(n // 4 + 1):
        er, ei = even[k]
        orr, oi = odd[k]
        if k == 0:
            out[0] = (er + orr, None)
            out[n // 2] = (er - orr, None)
        elif 4 * k == n:
            out[k] = (er, -orr)
        else:
            c, s = math.cos(2 * math.pi * k / n), math.sin(2 * math.pi * k / n)
            if 8 * k == n:
                tr, ti = (orr + oi) * c, (oi - orr) * c
            else:
                tr, ti = orr * c + oi * s, oi * c - orr * s
            out[k] = (er + tr, ei + ti)
            out[n // 2 - k] = (er - tr, ti - ei)
    return out


def pack_kernel(capacity, cells_per_dev, count_ref, dep_ref, weight_ref, cell_ref, out_ref):
    groups = out_ref.shape[0]
    lane = lax.broadcasted_iota(I32, (SUB, LANES), 1)
    for q in range(groups):
        tile = q // 2
        weight = weight_ref[:, tile * LANES : (tile + 1) * LANES]
        cells = jnp.broadcast_to(cell_ref[tile : tile + 1, :], (SUB, LANES))
        cells = (cells - q * cells_per_dev).astype(F32)
        if q % 2:
            weight = pltpu.roll(weight, capacity, 1)
        else:
            cells = pltpu.roll(cells, capacity, 1)
        live = jnp.where(lane < count_ref[q], 1.0, 0.0)
        out_ref[q, :capacity, :] = dep_ref[q * capacity : (q + 1) * capacity, :]
        out_ref[q, capacity:, :] = jnp.where(lane < capacity, weight * live, cells)


def pack(obs_count, departure, obs_weight, obs_cell, cells_per_dev):
    groups = obs_count.shape[0]
    slots = departure.shape[0]
    capacity = slots // groups
    assert 2 * capacity == LANES and obs_weight.shape[0] == SUB

    return pl.pallas_call(
        functools.partial(pack_kernel, capacity, cells_per_dev),
        out_shape=jax.ShapeDtypeStruct((groups, capacity + SUB, LANES), F32),
        in_specs=[
            pl.BlockSpec(memory_space=pltpu.SMEM),
            pl.BlockSpec(memory_space=pltpu.VMEM),
            pl.BlockSpec(memory_space=pltpu.VMEM),
            pl.BlockSpec(memory_space=pltpu.VMEM),
        ],
        out_specs=pl.BlockSpec(memory_space=pltpu.VMEM),
        compiler_params=pltpu.CompilerParams(vmem_limit_bytes=16 * MIB),
        name="pack",
    )(obs_count, departure, obs_weight, obs_cell.reshape(slots // LANES, LANES))


STREAMS = 4


def grid_kernel(
    recv_ref, gain_hbm, thi_hbm, tlo_hbm, pick_hbm, out_ref,
    *scratch,
):
    acc = scratch[:STREAMS]
    (gain, thi, tlo, pick, cells_v, cells_s, yhi, ylo, zhi, zlo, sems) = scratch[STREAMS:]
    groups, rows_in, _ = recv_ref.shape
    capacity = rows_in - SUB
    lat_dev = gain.shape[0]
    blocks = gain.shape[2] // LANES
    loads = [
        pltpu.make_async_copy(src, dst, sems.at[i])
        for i, (src, dst) in enumerate(
            ((gain_hbm, gain), (thi_hbm, thi), (tlo_hbm, tlo), (pick_hbm, pick))
        )
    ]
    for copy in loads:
        copy.start()
    cells_v[...] = recv_ref[:, capacity, :].astype(I32)
    cell_copy = pltpu.make_async_copy(cells_v, cells_s, sems.at[4])
    cell_copy.start()

    def clear(i, carry):
        for a in acc:
            a[pl.ds(i * SUB, SUB)] = jnp.zeros((SUB, SUB, LANES), F32)
        return carry

    lax.fori_loop(0, acc[0].shape[0] // SUB, clear, 0)
    cell_copy.wait()

    def scatter(s, carry):
        weight = recv_ref[s, capacity:, :]
        for i in range(0, capacity, STREAMS):
            cells = [cells_s[s, capacity + i + t] for t in range(STREAMS)]
            old = [acc[t][cells[t]] for t in range(STREAMS)]
            new = []
            for t in range(STREAMS):
                k = i + t
                wide = jnp.broadcast_to(weight[:, k : k + 1], (SUB, LANES))
                new.append(old[t] + wide * recv_ref[s, k : k + 1, :])
            for t in range(STREAMS):
                acc[t][cells[t]] = new[t]
        return carry

    lax.fori_loop(0, groups, scatter, 0)
    for copy in loads[:1]:
        copy.wait()

    width = blocks // RADIX * LANES
    pair = 2

    def transform(i, carry):
        r0 = i * pair
        for h in range(blocks // RADIX):
            xs = []
            for a in range(RADIX):
                b = a * (blocks // RADIX) + h
                parts = []
                for r in range(pair):
                    cell = (r0 + r) * blocks + b
                    total = acc[0][cell]
                    for t in range(1, STREAMS):
                        total = total + acc[t][cell]
                    parts.append(total * gain[r0 + r, :, b * LANES : (b + 1) * LANES])
                xs.append(jnp.concatenate(parts, axis=0))
            ys = real_fft(xs)
            rows = pl.ds(pl.multiple_of(r0 * SUB, pair * SUB), pair * SUB)
            for g in range(GROUPS):
                re, im = ys[g] if g else (ys[0][0], ys[RADIX // 2][0])
                for part, value in enumerate((re, im)):
                    lanes = pl.ds(part * width + h * LANES, LANES)
                    hi, lo = split(value)
                    yhi[g, rows, lanes] = hi
                    ylo[g, rows, lanes] = lo
        return carry

    lax.fori_loop(0, lat_dev // pair, transform, 0)
    for copy in loads[1:]:
        copy.wait()

    def dot(a, b):
        return jnp.dot(a, b, preferred_element_type=F32)

    for g in range(GROUPS):
        high = yhi[g]
        z = dot(high, thi[g]) + (dot(high, tlo[g]) + dot(ylo[g], thi[g]))
        re = z[:, :LANES].reshape(lat_dev, 1, SUB, LANES)
        im = z[:, LANES:].reshape(lat_dev, 1, SUB, LANES)
        both = jnp.concatenate([re, im], axis=1).reshape(lat_dev * 2 * SUB, LANES)
        hi, lo = split(both)
        zhi[:, g * LANES : (g + 1) * LANES] = hi
        zlo[:, g * LANES : (g + 1) * LANES] = lo

    dims = (((1,), (1,)), ((), ()))
    chunks = zhi.shape[0] // LANES
    tall = 128
    for j0 in range(0, pick.shape[0], tall):
        sel = pick[j0 : j0 + tall, :]
        res = lax.dot_general(sel, zhi[...], dims, preferred_element_type=F32)
        res = res + lax.dot_general(sel, zlo[...], dims, preferred_element_type=F32)
        for jt in range(tall // SUB):
            for c in range(chunks):
                start = (j0 + jt * SUB) * chunks + c
                out_ref[pl.ds(start, SUB, stride=chunks), :] = res[
                    jt * SUB : (jt + 1) * SUB, c * LANES : (c + 1) * LANES
                ]


def grid_to_waves(recv, gain, thi, tlo, pick):
    lat_dev, ch_dev, lon_count = gain.shape
    waves = pick.shape[0]
    cells = lat_dev * lon_count // LANES
    rows = lat_dev * ch_dev
    any_spec = pl.BlockSpec(memory_space=pl.ANY)
    return pl.pallas_call(
        grid_kernel,
        out_shape=jax.ShapeDtypeStruct((waves * 2 * rows // LANES, LANES), F32),
        in_specs=[pl.BlockSpec(memory_space=pltpu.VMEM)] + [any_spec] * 4,
        out_specs=pl.BlockSpec(memory_space=pltpu.VMEM),
        scratch_shapes=[pltpu.VMEM((cells, ch_dev, LANES), F32) for _ in range(STREAMS)]
        + [
            pltpu.VMEM(gain.shape, F32),
            pltpu.VMEM(thi.shape, BF16),
            pltpu.VMEM(tlo.shape, BF16),
            pltpu.VMEM(pick.shape, BF16),
            pltpu.VMEM((recv.shape[0], LANES), I32),
            pltpu.SMEM((recv.shape[0], LANES), I32),
            pltpu.VMEM((GROUPS, rows, thi.shape[1]), BF16),
            pltpu.VMEM((GROUPS, rows, thi.shape[1]), BF16),
            pltpu.VMEM((2 * rows, GROUPS * LANES), BF16),
            pltpu.VMEM((2 * rows, GROUPS * LANES), BF16),
            pltpu.SemaphoreType.DMA((5,)),
        ],
        compiler_params=pltpu.CompilerParams(vmem_limit_bytes=56 * MIB),
        name="grid_to_waves",
    )(recv, gain, thi, tlo, pick)


def prepare_kernel(lat_dev, band_ref, table_ref, hi_ref, lo_ref):
    grid_count = band_ref.shape[0]
    chunks = lat_dev // SUB
    half = 2 * SUB

    def body(c, carry):
        starts = [
            pl.multiple_of(band_ref[g] * lat_dev + c * SUB, SUB) for g in range(grid_count)
        ]
        for t in range(table_ref.shape[2] // LANES):
            lanes = pl.ds(t * LANES, LANES)
            for g0 in range(0, grid_count, half):
                turned = []
                for g1 in range(g0, g0 + half, SUB):
                    tiles = [
                        table_ref[0, pl.ds(starts[g], SUB), lanes] for g in range(g1, g1 + SUB)
                    ]
                    turned.append(jnp.swapaxes(jnp.stack(tiles), 0, 1))
                for k in range(SUB):
                    hi, lo = split(jnp.concatenate([x[k] for x in turned], axis=0))
                    start = pl.multiple_of((k * chunks + c) * grid_count + g0, half)
                    hi_ref[0, pl.ds(start, half), lanes] = hi
                    lo_ref[0, pl.ds(start, half), lanes] = lo
        return carry

    lax.fori_loop(0, chunks, body, 0)


def prepare_table(legendre, band_of, lat_dev):
    slot_count, lat_total, total_count = legendre.shape
    block = pl.BlockSpec((1, lat_total, total_count), lambda s: (s, 0, 0))
    return pl.pallas_call(
        functools.partial(prepare_kernel, lat_dev),
        grid=(slot_count,),
        out_shape=[jax.ShapeDtypeStruct(legendre.shape, BF16)] * 2,
        in_specs=[pl.BlockSpec(memory_space=pltpu.SMEM), block],
        out_specs=[block, block],
        compiler_params=pltpu.CompilerParams(vmem_limit_bytes=32 * MIB),
        cost_estimate=pl.CostEstimate(
            flops=4 * legendre.size, bytes_accessed=8 * legendre.size, transcendentals=0
        ),
        name="prepare_table",
    )(band_of, legendre)


def legendre_kernel(geo, x_ref, lhi_ref, llo_ref, out_ref):
    grid_count, lev_count, slot_count, chunks = geo
    slot = pl.program_id(0)
    lhs = []
    for lev in range(lev_count):
        pieces = []
        for c in range(chunks):
            start = (lev * slot_count + slot) * chunks + c
            pieces.append(
                x_ref[pl.ds(start, grid_count, stride=lev_count * slot_count * chunks), :]
            )
        lhs.append(jnp.concatenate(pieces, axis=0).T)
    depth = chunks * grid_count
    wide = 2 * SUB
    total = None
    for k in range(LANES // wide):
        part = jnp.concatenate([m[k * wide : (k + 1) * wide] for m in lhs], axis=0)
        hi, lo = split(part)
        both = jnp.concatenate([hi, lo], axis=0)
        rows = pl.ds(k * depth, depth)
        prod = jnp.dot(both, lhi_ref[0, rows, :], preferred_element_type=F32)
        prod = prod[: hi.shape[0]] + (
            prod[hi.shape[0] :]
            + jnp.dot(hi, llo_ref[0, rows, :], preferred_element_type=F32)
        )
        total = prod if total is None else total + prod
    tiles = total.shape[1] // LANES
    for lev in range(lev_count):
        for p in range(2):
            row = lev * wide + p * SUB
            for t in range(tiles):
                start = lev * SUB * tiles * 2 + t * 2 + p
                out_ref[0, pl.ds(start, SUB, stride=tiles * 2), :] = total[
                    row : row + SUB, t * LANES : (t + 1) * LANES
                ]


def legendre_step(waves, lhi, llo, grid_count, lev_count):

    slot_count, lat_total, total_count = lhi.shape
    chunks = waves.shape[0] // (grid_count * lev_count * slot_count)
    geo = (grid_count, lev_count, slot_count, chunks)
    out_rows = lev_count * SUB * 2 * total_count // LANES
    return pl.pallas_call(
        functools.partial(legendre_kernel, geo),
        grid=(slot_count,),
        out_shape=jax.ShapeDtypeStruct((slot_count, out_rows, LANES), F32),
        in_specs=[
            pl.BlockSpec(waves.shape, lambda s: (0, 0)),
            pl.BlockSpec((1, lat_total, total_count), lambda s: (s, 0, 0)),
            pl.BlockSpec((1, lat_total, total_count), lambda s: (s, 0, 0)),
        ],
        out_specs=pl.BlockSpec((1, out_rows, LANES), lambda s: (s, 0, 0)),
        compiler_params=pltpu.CompilerParams(vmem_limit_bytes=40 * MIB),
        name="legendre_step",
    )(waves, lhi, llo)


def shards(trajectory, legendre, obs_cell, obs_count, departure, obs_weight, band_of, m_order):
    grid_count = lax.axis_size("grid")
    lev_count = lax.axis_size("lev")
    ch_dev, lat_dev, lon_count = trajectory.shape
    slot_count, lat_total, total_count = legendre.shape
    wave_total = m_order.shape[0]
    cells_per_dev = lat_dev * lon_count // LANES

    sent = pack(obs_count, departure, obs_weight, obs_cell, cells_per_dev)
    recv = lax.all_to_all(sent, "grid", split_axis=0, concat_axis=0, tiled=True)

    gain = jnp.swapaxes(1.0 + 0.5 * jnp.tanh(trajectory), 0, 1)
    thi, tlo = split_np(wave_table(wave_total, lon_count))
    cols = wave_columns(wave_total).reshape(1, -1)
    pick = (m_order[:, None] == cols).astype(BF16)

    waves = grid_to_waves(recv, gain, jnp.asarray(thi), jnp.asarray(tlo), pick)
    outgoing = waves.reshape(grid_count * lev_count, 1, -1)
    incoming = lax.all_to_all(
        outgoing, ("grid", "lev"), split_axis=0, concat_axis=0, tiled=True
    )

    lhi, llo = prepare_table(legendre, band_of, lat_dev)
    out = legendre_step(incoming.reshape(-1, LANES), lhi, llo, grid_count, lev_count)
    tiles = total_count // LANES
    out = out.reshape(slot_count, lev_count * ch_dev, tiles, 2, LANES)
    return jnp.swapaxes(out, 2, 3).reshape(slot_count, lev_count * ch_dev, 2, total_count)


def solution(mesh):
    placed = (
        P("lev", "grid", None),
        P(("grid", "lev"), None, None),
        P("grid"),
        P("grid"),
        P("grid", None),
        P("lev", "grid"),
        P(),
        P(),
    )
    return jax.shard_map(
        shards,
        mesh=mesh,
        in_specs=placed,
        out_specs=P(("grid", "lev"), None, None, None),
        check_vma=False,
    )
```

```python
import functools
import math

import jax
import jax.numpy as jnp
import numpy as np
from jax import lax
from jax.experimental import pallas as pl
from jax.experimental.pallas import tpu as pltpu
from jax.sharding import PartitionSpec as P

LANES = 128
SUB = 8
RADIX = 16
GROUPS = RADIX // 2
MIB = 1 << 20
F32 = jnp.float32
BF16 = jnp.bfloat16
I32 = jnp.int32


def wave_columns(wave_total):
    per_residue = wave_total // RADIX
    cols = np.zeros((GROUPS, 2 * per_residue), np.int32)
    for g in range(GROUPS):
        first, second = g, (RADIX - g if g else RADIX // 2)
        turns = RADIX * np.arange(per_residue)
        cols[g, :per_residue] = first + turns
        cols[g, per_residue : 2 * per_residue] = second + turns
    return cols


def wave_table(wave_total, lon_count):
    width = lon_count // RADIX
    cols = wave_columns(wave_total)
    per_residue = wave_total // RADIX
    fine = np.arange(width, dtype=np.int64)
    out = np.zeros((GROUPS, 2, width, 2, LANES), np.float64)
    for g in range(GROUPS):
        for i in range(2 * per_residue):
            m = int(cols[g, i])
            lane = (g * 2 * per_residue + i) % LANES
            angle = 2.0 * math.pi / lon_count * ((m * fine) % lon_count)
            factor = 1.0 if m == 0 else 2.0
            cos, sin = factor * np.cos(angle), factor * np.sin(angle)
            second = i >= per_residue
            if g == 0:
                part = 1 if second else 0
                out[g, part, :, 0, lane] = cos
                out[g, part, :, 1, lane] = -sin
            else:
                sign = -1.0 if second else 1.0
                out[g, 0, :, 0, lane] = cos
                out[g, 1, :, 0, lane] = sign * sin
                out[g, 0, :, 1, lane] = -sin
                out[g, 1, :, 1, lane] = sign * cos
    return out.reshape(GROUPS, 2 * width, 2 * LANES).astype(np.float32)


def split_np(table):
    high = table.astype(jnp.bfloat16)
    low = (table - high.astype(np.float32)).astype(jnp.bfloat16)
    return high, low


def split(x):
    high = x.astype(BF16)
    return high, (x - high.astype(F32)).astype(BF16)


def real_fft(xs):
    n = len(xs)
    if n == 2:
        return [(xs[0] + xs[1], None), (xs[0] - xs[1], None)]
    even, odd = real_fft(xs[0::2]), real_fft(xs[1::2])
    out = [None] * (n // 2 + 1)
    for k in range(n // 4 + 1):
        er, ei = even[k]
        orr, oi = odd[k]
        if k == 0:
            out[0] = (er + orr, None)
            out[n // 2] = (er - orr, None)
        elif 4 * k == n:
            out[k] = (er, -orr)
        else:
            c, s = math.cos(2 * math.pi * k / n), math.sin(2 * math.pi * k / n)
            if 8 * k == n:
                tr, ti = (orr + oi) * c, (oi - orr) * c
            else:
                tr, ti = orr * c + oi * s, oi * c - orr * s
            out[k] = (er + tr, ei + ti)
            out[n // 2 - k] = (er - tr, ti - ei)
    return out


def pack_kernel(
    capacity, cells_per_dev, count_hbm, dep_hbm, weight_hbm, cell_hbm, out_ref,
    counts, weights, cells_v, sems,
):
    groups = out_ref.shape[0]
    small = [
        pltpu.make_async_copy(src, dst, sems.at[i])
        for i, (src, dst) in enumerate(
            ((count_hbm, counts), (weight_hbm, weights), (cell_hbm, cells_v))
        )
    ]
    for copy in small:
        copy.start()
    parts = 4
    each = groups // parts
    large = [
        pltpu.make_async_copy(
            dep_hbm.at[pl.ds(i * each, each)],
            out_ref.at[pl.ds(i * each, each), pl.ds(0, capacity)],
            sems.at[3 + i],
        )
        for i in range(parts)
    ]
    for copy in large:
        copy.start()
    for copy in small:
        copy.wait()
    lane = lax.broadcasted_iota(I32, (SUB, LANES), 1)
    for q in range(groups):
        tile = q // 2
        weight = weights[:, tile * LANES : (tile + 1) * LANES]
        cells = jnp.broadcast_to(cells_v[tile : tile + 1, :], (SUB, LANES))
        cells = (cells - q * cells_per_dev).astype(F32)
        if q % 2:
            weight = pltpu.roll(weight, capacity, 1)
        else:
            cells = pltpu.roll(cells, capacity, 1)
        live = jnp.where(lane < counts[q], 1.0, 0.0)
        out_ref[q, capacity:, :] = jnp.where(lane < capacity, weight * live, cells)
    for copy in large:
        copy.wait()


def pack(obs_count, departure, obs_weight, obs_cell, cells_per_dev):
    groups = obs_count.shape[0]
    slots = departure.shape[0]
    capacity = slots // groups
    assert 2 * capacity == LANES and obs_weight.shape[0] == SUB
    cell_rows = obs_cell.reshape(slots // LANES, LANES)
    return pl.pallas_call(
        functools.partial(pack_kernel, capacity, cells_per_dev),
        out_shape=jax.ShapeDtypeStruct((groups, capacity + SUB, LANES), F32),
        in_specs=[pl.BlockSpec(memory_space=pltpu.HBM)] * 4,
        out_specs=pl.BlockSpec(memory_space=pltpu.VMEM),
        scratch_shapes=[
            pltpu.SMEM(obs_count.shape, I32),
            pltpu.VMEM(obs_weight.shape, F32),
            pltpu.VMEM(cell_rows.shape, I32),
            pltpu.SemaphoreType.DMA((7,)),
        ],
        compiler_params=pltpu.CompilerParams(vmem_limit_bytes=60 * MIB),
        name="pack",
    )(obs_count, departure.reshape(groups, capacity, LANES), obs_weight, cell_rows)


STREAMS = 4


def grid_kernel(
    recv_hbm, gain_hbm, thi_hbm, tlo_hbm, pick_hbm, out_hbm, *scratch
):
    acc = scratch[:STREAMS]
    (recv, extra, gain, thi, tlo, pick, cells_v, cells_s, wide, yhi, ylo, zt, out, sems) = scratch[
        STREAMS:
    ]
    groups, capacity, _ = recv.shape
    lat_dev = gain.shape[0]
    blocks = gain.shape[2] // LANES
    first = pltpu.make_async_copy(recv_hbm.at[:, pl.ds(capacity, SUB)], extra, sems.at[0])
    first.start()
    parts = 4
    each = groups // parts
    deps = [
        pltpu.make_async_copy(
            recv_hbm.at[pl.ds(i * each, each), pl.ds(0, capacity)],
            recv.at[pl.ds(i * each, each)],
            sems.at[2 + i],
        )
        for i in range(parts)
    ]
    half = lat_dev // 2
    loads = [
        pltpu.make_async_copy(src, dst, sems.at[2 + parts + i])
        for i, (src, dst) in enumerate(
            (
                (gain_hbm.at[pl.ds(0, half)], gain.at[pl.ds(0, half)]),
                (gain_hbm.at[pl.ds(half, half)], gain.at[pl.ds(half, half)]),
                (thi_hbm, thi),
                (tlo_hbm, tlo),
                (pick_hbm, pick),
            )
        )
    ]
    for copy in deps:
        copy.start()

    def clear(i, carry):
        for a in acc:
            a[pl.ds(i * SUB, SUB)] = jnp.zeros((SUB, SUB, LANES), F32)
        return carry

    lax.fori_loop(0, acc[0].shape[0] // SUB, clear, 0)

    first.wait()
    cells_v[...] = extra[:, 0, :].astype(I32)
    cell_copy = pltpu.make_async_copy(cells_v, cells_s, sems.at[1])
    cell_copy.start()

    rows = groups * SUB
    weight = extra[...].reshape(rows, LANES)
    lane = lax.broadcasted_iota(I32, (rows, LANES), 1)
    whi, wlo = split(weight)
    both = jnp.where(
        lane < capacity, whi.astype(F32), pltpu.roll(wlo.astype(F32), capacity, 1)
    ).astype(BF16)
    row = lax.broadcasted_iota(I32, (LANES, 2 * LANES), 0) % capacity
    col = lax.broadcasted_iota(I32, (LANES, 2 * LANES), 1) // LANES
    offset = row - col

    def widen(i, carry):
        ones = jnp.where(offset == 2 * i, 1.0, 0.0).astype(BF16)
        res = jnp.dot(both, ones, preferred_element_type=F32)
        wide[2 * i] = res[:, :LANES]
        wide[2 * i + 1] = res[:, LANES:]
        return carry

    lax.fori_loop(0, capacity // 2, widen, 0, unroll=4)
    cell_copy.wait()

    for copy in deps:
        copy.wait()
    for copy in loads:
        copy.start()

    def scatter(s, carry):
        w_rows = pl.ds(pl.multiple_of(s * SUB, SUB), SUB)
        for i in range(0, capacity, STREAMS):
            cells = [cells_s[s, capacity + i + t] for t in range(STREAMS)]
            old = [acc[t][cells[t]] for t in range(STREAMS)]
            new = []
            for t in range(STREAMS):
                k = i + t
                new.append(old[t] + wide[k, w_rows, :] * recv[s, k : k + 1, :])
            for t in range(STREAMS):
                acc[t][cells[t]] = new[t]
        return carry

    lax.fori_loop(0, groups, scatter, 0)
    for copy in loads[:2]:
        copy.wait()

    width = blocks // RADIX * LANES
    pair = 2

    def transform(i, carry):
        r0 = i * pair
        for h in range(blocks // RADIX):
            xs = []
            for a in range(RADIX):
                b = a * (blocks // RADIX) + h
                parts = []
                for r in range(pair):
                    cell = (r0 + r) * blocks + b
                    total = acc[0][cell]
                    for t in range(1, STREAMS):
                        total = total + acc[t][cell]
                    parts.append(total * gain[r0 + r, :, b * LANES : (b + 1) * LANES])
                xs.append(jnp.concatenate(parts, axis=0))
            ys = real_fft(xs)
            rows = pl.ds(pl.multiple_of(r0 * SUB, pair * SUB), pair * SUB)
            for g in range(GROUPS):
                re, im = ys[g] if g else (ys[0][0], ys[RADIX // 2][0])
                for part, value in enumerate((re, im)):
                    lanes = pl.ds(part * width + h * LANES, LANES)
                    hi, lo = split(value)
                    yhi[g, rows, lanes] = hi
                    ylo[g, rows, lanes] = lo
        return carry

    lax.fori_loop(0, lat_dev // pair, transform, 0)
    for copy in loads[2:]:
        copy.wait()

    def dot(a, b):
        return jnp.dot(a, b, preferred_element_type=F32)

    waves = pick.shape[0]
    members = waves // GROUPS
    lane = lax.broadcasted_iota(I32, (2 * lat_dev * SUB, LANES), 1)
    open_tile = None
    for g in range(GROUPS):
        high = yhi[g]
        z = dot(high, thi[g]) + (dot(high, tlo[g]) + dot(ylo[g], thi[g]))
        re = z[:, :LANES].reshape(lat_dev, 1, SUB, LANES)
        im = z[:, LANES:].reshape(lat_dev, 1, SUB, LANES)
        both = jnp.concatenate([re, im], axis=1).reshape(lat_dev * 2 * SUB, LANES)
        tile, offset = divmod(g * members, LANES)
        past = offset + members - LANES
        mine = jnp.where(lane >= offset, both, 0.0) if past > 0 else both
        open_tile = mine if open_tile is None else open_tile + mine
        if past >= 0:
            hi, lo = split(open_tile.T)
            zt[tile * LANES : (tile + 1) * LANES, :] = hi
            zt[waves + tile * LANES : waves + (tile + 1) * LANES, :] = lo
            open_tile = jnp.where(lane < past, both, 0.0) if past > 0 else None

    chunks = zt.shape[1] // LANES
    tall = LANES
    sends = []
    for j0 in range(0, waves, tall):
        sel = pick[j0 : j0 + tall, :]
        res = dot(jnp.concatenate([sel, sel], axis=1), zt[...])
        for jt in range(tall // SUB):
            for c in range(chunks):
                start = (j0 + jt * SUB) * chunks + c
                out[pl.ds(start, SUB, stride=chunks), :] = res[
                    jt * SUB : (jt + 1) * SUB, c * LANES : (c + 1) * LANES
                ]
        span = pl.ds(j0 * chunks, tall * chunks)
        sends.append(
            pltpu.make_async_copy(out.at[span], out_hbm.at[span], sems.at[11 + j0 // tall])
        )
        sends[-1].start()
    for copy in sends:
        copy.wait()


def grid_to_waves(recv, gain, thi, tlo, pick):
    lat_dev, ch_dev, lon_count = gain.shape
    waves = pick.shape[0]
    groups, capacity = recv.shape[0], recv.shape[1] - SUB
    cells = lat_dev * lon_count // LANES
    rows = lat_dev * ch_dev
    return pl.pallas_call(
        grid_kernel,
        out_shape=jax.ShapeDtypeStruct((waves * 2 * rows // LANES, LANES), F32),
        in_specs=[pl.BlockSpec(memory_space=pltpu.HBM)] * 5,
        out_specs=pl.BlockSpec(memory_space=pltpu.HBM),
        scratch_shapes=[pltpu.VMEM((cells, ch_dev, LANES), F32) for _ in range(STREAMS)]
        + [
            pltpu.VMEM((groups, capacity, LANES), F32),
            pltpu.VMEM((groups, SUB, LANES), F32),
            pltpu.VMEM(gain.shape, F32),
            pltpu.VMEM(thi.shape, BF16),
            pltpu.VMEM(tlo.shape, BF16),
            pltpu.VMEM(pick.shape, BF16),
            pltpu.VMEM((groups, LANES), I32),
            pltpu.SMEM((groups, LANES), I32),
            pltpu.VMEM((capacity, groups * SUB, LANES), F32),
            pltpu.VMEM((GROUPS, rows, thi.shape[1]), BF16),
            pltpu.VMEM((GROUPS, rows, thi.shape[1]), BF16),
            pltpu.VMEM((2 * waves, 2 * rows), BF16),
            pltpu.VMEM((waves * 2 * rows // LANES, LANES), F32),
            pltpu.SemaphoreType.DMA((11 + waves // LANES,)),
        ],
        compiler_params=pltpu.CompilerParams(vmem_limit_bytes=60 * MIB),
        name="grid_to_waves",
    )(recv, gain, thi, tlo, pick)


def prepare_kernel(lat_dev, band_ref, table_ref, hi_ref, lo_ref):
    grid_count = band_ref.shape[0]
    chunks = lat_dev // SUB
    half = 2 * SUB

    def body(c, carry):
        starts = [
            pl.multiple_of(band_ref[g] * lat_dev + c * SUB, SUB) for g in range(grid_count)
        ]
        for t in range(table_ref.shape[2] // LANES):
            lanes = pl.ds(t * LANES, LANES)
            for g0 in range(0, grid_count, half):
                turned = []
                for g1 in range(g0, g0 + half, SUB):
                    tiles = [
                        table_ref[0, pl.ds(starts[g], SUB), lanes] for g in range(g1, g1 + SUB)
                    ]
                    turned.append(jnp.swapaxes(jnp.stack(tiles), 0, 1))
                for k in range(SUB):
                    hi, lo = split(jnp.concatenate([x[k] for x in turned], axis=0))
                    start = pl.multiple_of((k * chunks + c) * grid_count + g0, half)
                    hi_ref[0, pl.ds(start, half), lanes] = hi
                    lo_ref[0, pl.ds(start, half), lanes] = lo
        return carry

    lax.fori_loop(0, chunks, body, 0)


def prepare_table(legendre, band_of, lat_dev):
    slot_count, lat_total, total_count = legendre.shape
    block = pl.BlockSpec((1, lat_total, total_count), lambda s: (s, 0, 0))
    return pl.pallas_call(
        functools.partial(prepare_kernel, lat_dev),
        grid=(slot_count,),
        out_shape=[jax.ShapeDtypeStruct(legendre.shape, BF16)] * 2,
        in_specs=[pl.BlockSpec(memory_space=pltpu.SMEM), block],
        out_specs=[block, block],
        compiler_params=pltpu.CompilerParams(vmem_limit_bytes=56 * MIB),
        cost_estimate=pl.CostEstimate(
            flops=4 * legendre.size, bytes_accessed=8 * legendre.size, transcendentals=0
        ),
        name="prepare_table",
    )(band_of, legendre)


def legendre_kernel(geo, x_hbm, lhi_hbm, llo_hbm, out_hbm, x_ref, lhi, llo, out, sems):
    grid_count, lev_count, slot_count, chunks = geo
    depth = chunks * grid_count
    wide = 2 * SUB
    first = pltpu.make_async_copy(x_hbm, x_ref, sems.at[0])
    first.start()

    def loads(slot):
        return [
            pltpu.make_async_copy(src.at[slot], dst.at[slot], sems.at[1 + 2 * slot + i])
            for i, (src, dst) in enumerate(((lhi_hbm, lhi), (llo_hbm, llo)))
        ]

    for slot in range(slot_count):
        for copy in loads(slot):
            copy.start()
    first.wait()

    def store(slot):
        return pltpu.make_async_copy(
            out.at[slot], out_hbm.at[slot], sems.at[1 + 2 * slot_count + slot]
        )

    def body(slot, carry):
        lhs = []
        for lev in range(lev_count):
            pieces = []
            for c in range(chunks):
                start = (lev * slot_count + slot) * chunks + c
                pieces.append(
                    x_ref[pl.ds(start, grid_count, stride=lev_count * slot_count * chunks), :]
                )
            lhs.append(jnp.concatenate(pieces, axis=0).T)
        for copy in loads(slot):
            copy.wait()
        total = None
        for k in range(LANES // wide):
            part = jnp.concatenate([m[k * wide : (k + 1) * wide] for m in lhs], axis=0)
            hi, lo = split(part)
            both = jnp.concatenate([hi, lo], axis=0)
            rows = pl.ds(k * depth, depth)
            prod = jnp.dot(both, lhi[slot, rows, :], preferred_element_type=F32)
            prod = prod[: hi.shape[0]] + (
                prod[hi.shape[0] :]
                + jnp.dot(hi, llo[slot, rows, :], preferred_element_type=F32)
            )
            total = prod if total is None else total + prod
        for lev in range(lev_count):
            re = total[lev * wide : lev * wide + SUB]
            im = total[lev * wide + SUB : (lev + 1) * wide]
            out[slot, lev * SUB : (lev + 1) * SUB] = jnp.stack([re, im], axis=1)
        store(slot).start()
        return carry

    lax.fori_loop(0, slot_count, body, 0)
    for slot in range(slot_count):
        store(slot).wait()


def legendre_step(waves, lhi, llo, grid_count, lev_count):
    slot_count, lat_total, total_count = lhi.shape
    chunks = waves.shape[0] // (grid_count * lev_count * slot_count)
    geo = (grid_count, lev_count, slot_count, chunks)
    out_shape = (slot_count, lev_count * SUB, 2, total_count)
    return pl.pallas_call(
        functools.partial(legendre_kernel, geo),
        out_shape=jax.ShapeDtypeStruct(out_shape, F32),
        in_specs=[pl.BlockSpec(memory_space=pltpu.HBM)] * 3,
        out_specs=pl.BlockSpec(memory_space=pltpu.HBM),
        scratch_shapes=[
            pltpu.VMEM(waves.shape, F32),
            pltpu.VMEM(lhi.shape, BF16),
            pltpu.VMEM(llo.shape, BF16),
            pltpu.VMEM(out_shape, F32),
            pltpu.SemaphoreType.DMA((1 + 3 * slot_count,)),
        ],
        compiler_params=pltpu.CompilerParams(vmem_limit_bytes=60 * MIB),
        name="legendre_step",
    )(waves, lhi, llo)


def shards(trajectory, legendre, obs_cell, obs_count, departure, obs_weight, band_of, m_order):
    grid_count = lax.axis_size("grid")
    lev_count = lax.axis_size("lev")
    ch_dev, lat_dev, lon_count = trajectory.shape
    slot_count, lat_total, total_count = legendre.shape
    wave_total = m_order.shape[0]
    cells_per_dev = lat_dev * lon_count // LANES

    sent = pack(obs_count, departure, obs_weight, obs_cell, cells_per_dev)
    recv = lax.all_to_all(sent, "grid", split_axis=0, concat_axis=0, tiled=True)

    gain = jnp.swapaxes(1.0 + 0.5 * jnp.tanh(trajectory), 0, 1)
    thi, tlo = split_np(wave_table(wave_total, lon_count))
    cols = wave_columns(wave_total).reshape(1, -1)
    pick = (m_order[:, None] == cols).astype(BF16)

    waves = grid_to_waves(recv, gain, jnp.asarray(thi), jnp.asarray(tlo), pick)
    outgoing = waves.reshape(grid_count * lev_count, 1, -1)
    incoming = lax.all_to_all(
        outgoing, ("grid", "lev"), split_axis=0, concat_axis=0, tiled=True
    )

    lhi, llo = prepare_table(legendre, band_of, lat_dev)
    return legendre_step(
        incoming.reshape(-1, LANES), lhi, llo, grid_count, lev_count
    )


def solution(mesh):
    placed = (
        P("lev", "grid", None),
        P(("grid", "lev"), None, None),
        P("grid"),
        P("grid"),
        P("grid", None),
        P("lev", "grid"),
        P(),
        P(),
    )
    return jax.shard_map(
        shards,
        mesh=mesh,
        in_specs=placed,
        out_specs=P(("grid", "lev"), None, None, None),
        check_vma=False,
    )
```

```python
import functools
import math

import jax
import jax.numpy as jnp
import numpy as np
from jax import lax
from jax.experimental import pallas as pl
from jax.experimental.pallas import tpu as pltpu
from jax.sharding import PartitionSpec as P

LANES = 128
SUB = 8
RADIX = 16
GROUPS = RADIX // 2
MIB = 1 << 20
F32 = jnp.float32
BF16 = jnp.bfloat16
I32 = jnp.int32


def wave_columns(wave_total):
    per_residue = wave_total // RADIX
    cols = np.zeros((GROUPS, 2 * per_residue), np.int32)
    for g in range(GROUPS):
        first, second = g, (RADIX - g if g else RADIX // 2)
        turns = RADIX * np.arange(per_residue)
        cols[g, :per_residue] = first + turns
        cols[g, per_residue : 2 * per_residue] = second + turns
    return cols


def wave_table(wave_total, lon_count):
    width = lon_count // RADIX
    cols = wave_columns(wave_total)
    per_residue = wave_total // RADIX
    fine = np.arange(width, dtype=np.int64)
    out = np.zeros((GROUPS, 2, width, 2, LANES), np.float64)
    for g in range(GROUPS):
        for i in range(2 * per_residue):
            m = int(cols[g, i])
            lane = (g * 2 * per_residue + i) % LANES
            angle = 2.0 * math.pi / lon_count * ((m * fine) % lon_count)
            factor = 1.0 if m == 0 else 2.0
            cos, sin = factor * np.cos(angle), factor * np.sin(angle)
            second = i >= per_residue
            if g == 0:
                part = 1 if second else 0
                out[g, part, :, 0, lane] = cos
                out[g, part, :, 1, lane] = -sin
            else:
                sign = -1.0 if second else 1.0
                out[g, 0, :, 0, lane] = cos
                out[g, 1, :, 0, lane] = sign * sin
                out[g, 0, :, 1, lane] = -sin
                out[g, 1, :, 1, lane] = sign * cos
    return out.reshape(GROUPS, 2 * width, 2 * LANES).astype(np.float32)


def split_np(table):
    high = table.astype(jnp.bfloat16)
    low = (table - high.astype(np.float32)).astype(jnp.bfloat16)
    return high, low


def split(x):
    high = x.astype(BF16)
    return high, (x - high.astype(F32)).astype(BF16)


def real_fft(xs):
    n = len(xs)
    if n == 2:
        return [(xs[0] + xs[1], None), (xs[0] - xs[1], None)]
    even, odd = real_fft(xs[0::2]), real_fft(xs[1::2])
    out = [None] * (n // 2 + 1)
    for k in range(n // 4 + 1):
        er, ei = even[k]
        orr, oi = odd[k]
        if k == 0:
            out[0] = (er + orr, None)
            out[n // 2] = (er - orr, None)
        elif 4 * k == n:
            out[k] = (er, -orr)
        else:
            c, s = math.cos(2 * math.pi * k / n), math.sin(2 * math.pi * k / n)
            if 8 * k == n:
                tr, ti = (orr + oi) * c, (oi - orr) * c
            else:
                tr, ti = orr * c + oi * s, oi * c - orr * s
            out[k] = (er + tr, ei + ti)
            out[n // 2 - k] = (er - tr, ti - ei)
    return out


def pack_kernel(
    capacity, cells_per_dev, count_hbm, dep_hbm, weight_hbm, cell_hbm, out_ref,
    counts, weights, cells_v, sems,
):
    groups = out_ref.shape[0]
    small = [
        pltpu.make_async_copy(src, dst, sems.at[i])
        for i, (src, dst) in enumerate(
            ((count_hbm, counts), (weight_hbm, weights), (cell_hbm, cells_v))
        )
    ]
    for copy in small:
        copy.start()
    parts = 4
    each = groups // parts
    large = [
        pltpu.make_async_copy(
            dep_hbm.at[pl.ds(i * each, each)],
            out_ref.at[pl.ds(i * each, each), pl.ds(0, capacity)],
            sems.at[3 + i],
        )
        for i in range(parts)
    ]
    for copy in large:
        copy.start()
    for copy in small:
        copy.wait()
    lane = lax.broadcasted_iota(I32, (SUB, LANES), 1)
    for q in range(groups):
        tile = q // 2
        weight = weights[:, tile * LANES : (tile + 1) * LANES]
        cells = jnp.broadcast_to(cells_v[tile : tile + 1, :], (SUB, LANES))
        cells = (cells - q * cells_per_dev).astype(F32)
        if q % 2:
            weight = pltpu.roll(weight, capacity, 1)
        else:
            cells = pltpu.roll(cells, capacity, 1)
        live = jnp.where(lane < counts[q], 1.0, 0.0)
        out_ref[q, capacity:, :] = jnp.where(lane < capacity, weight * live, cells)
    for copy in large:
        copy.wait()


def pack(obs_count, departure, obs_weight, obs_cell, cells_per_dev):
    groups = obs_count.shape[0]
    slots = departure.shape[0]
    capacity = slots // groups
    assert 2 * capacity == LANES and obs_weight.shape[0] == SUB
    cell_rows = obs_cell.reshape(slots // LANES, LANES)
    return pl.pallas_call(
        functools.partial(pack_kernel, capacity, cells_per_dev),
        out_shape=jax.ShapeDtypeStruct((groups, capacity + SUB, LANES), F32),
        in_specs=[pl.BlockSpec(memory_space=pltpu.HBM)] * 4,
        out_specs=pl.BlockSpec(memory_space=pltpu.VMEM),
        scratch_shapes=[
            pltpu.SMEM(obs_count.shape, I32),
            pltpu.VMEM(obs_weight.shape, F32),
            pltpu.VMEM(cell_rows.shape, I32),
            pltpu.SemaphoreType.DMA((7,)),
        ],
        compiler_params=pltpu.CompilerParams(vmem_limit_bytes=60 * MIB),
        name="pack",
    )(obs_count, departure.reshape(groups, capacity, LANES), obs_weight, cell_rows)


STREAMS = 4
AHEAD = 5


def grid_kernel(
    recv_hbm, gain_hbm, thi_hbm, tlo_hbm, pick_hbm, out_hbm, *scratch
):
    acc = scratch[:STREAMS]
    (recv, extra, gain, thi, tlo, pick, cells_v, cells_s, wide_a, wide_b, yhi, ylo, zt, out, sems) = scratch[
        STREAMS:
    ]
    groups, capacity, _ = recv.shape
    lat_dev = gain.shape[0]
    blocks = gain.shape[2] // LANES
    first = pltpu.make_async_copy(recv_hbm.at[:, pl.ds(capacity, SUB)], extra, sems.at[0])
    first.start()
    parts = 4
    each = groups // parts
    deps = [
        pltpu.make_async_copy(
            recv_hbm.at[pl.ds(i * each, each), pl.ds(0, capacity)],
            recv.at[pl.ds(i * each, each)],
            sems.at[2 + i],
        )
        for i in range(parts)
    ]
    half = lat_dev // 2
    loads = [
        pltpu.make_async_copy(src, dst, sems.at[2 + parts + i])
        for i, (src, dst) in enumerate(
            (
                (gain_hbm.at[pl.ds(0, half)], gain.at[pl.ds(0, half)]),
                (gain_hbm.at[pl.ds(half, half)], gain.at[pl.ds(half, half)]),
                (thi_hbm, thi),
                (tlo_hbm, tlo),
                (pick_hbm, pick),
            )
        )
    ]
    for copy in deps:
        copy.start()

    def clear(i, carry):
        for a in acc:
            a[pl.ds(i * SUB, SUB)] = jnp.zeros((SUB, SUB, LANES), F32)
        return carry

    lax.fori_loop(0, acc[0].shape[0] // SUB, clear, 0)

    first.wait()
    cells_v[...] = extra[:, 0, :].astype(I32)
    cell_copy = pltpu.make_async_copy(cells_v, cells_s, sems.at[1])
    cell_copy.start()

    rows = groups * SUB
    weight = extra[...].reshape(rows, LANES)
    lane = lax.broadcasted_iota(I32, (rows, LANES), 1)
    whi, wlo = split(weight)
    both = jnp.where(
        lane < capacity, whi.astype(F32), pltpu.roll(wlo.astype(F32), capacity, 1)
    ).astype(BF16)
    row = lax.broadcasted_iota(I32, (LANES, 2 * LANES), 0) % capacity
    col = lax.broadcasted_iota(I32, (LANES, 2 * LANES), 1) // LANES
    offset = row - col

    def widen(ref, k0):
        ones = jnp.where(offset == k0, 1.0, 0.0).astype(BF16)
        ref[...] = jnp.dot(both, ones, preferred_element_type=F32)

    def add_slots(ref, k0):
        per = STREAMS // 2
        for s0 in range(0, groups, per):
            slots = [(s0 + t // 2, t % 2) for t in range(STREAMS)]
            cells = [cells_s[s, capacity + k0 + kk] for s, kk in slots]
            old = [acc[t][cells[t]] for t in range(STREAMS)]
            new = []
            for t, (s, kk) in enumerate(slots):
                weights = ref[s * SUB : (s + 1) * SUB, kk * LANES : (kk + 1) * LANES]
                new.append(old[t] + weights * recv[s, pl.ds(k0 + kk, 1), :])
            for t in range(STREAMS):
                acc[t][cells[t]] = new[t]

    widen(wide_a, 0)
    cell_copy.wait()
    for copy in deps:
        copy.wait()
    for copy in loads:
        copy.start()

    def scatter(i, carry):
        k0 = 4 * i
        widen(wide_b, k0 + 2)
        add_slots(wide_a, k0)
        widen(wide_a, k0 + 4)
        add_slots(wide_b, k0 + 2)
        return carry

    lax.fori_loop(0, capacity // 4, scatter, 0)
    for copy in loads[:2]:
        copy.wait()

    width = blocks // RADIX * LANES
    pair = 2

    def transform(i, carry):
        r0 = i * pair
        for h in range(blocks // RADIX):
            xs = []
            for a in range(RADIX):
                b = a * (blocks // RADIX) + h
                parts = []
                for r in range(pair):
                    cell = (r0 + r) * blocks + b
                    total = acc[0][cell]
                    for t in range(1, STREAMS):
                        total = total + acc[t][cell]
                    parts.append(total * gain[r0 + r, :, b * LANES : (b + 1) * LANES])
                xs.append(jnp.concatenate(parts, axis=0))
            ys = real_fft(xs)
            rows = pl.ds(pl.multiple_of(r0 * SUB, pair * SUB), pair * SUB)
            for g in range(GROUPS):
                re, im = ys[g] if g else (ys[0][0], ys[RADIX // 2][0])
                for part, value in enumerate((re, im)):
                    lanes = pl.ds(part * width + h * LANES, LANES)
                    hi, lo = split(value)
                    yhi[g, rows, lanes] = hi
                    ylo[g, rows, lanes] = lo
        return carry

    lax.fori_loop(0, lat_dev // pair, transform, 0)
    for copy in loads[2:]:
        copy.wait()

    def dot(a, b):
        return jnp.dot(a, b, preferred_element_type=F32)

    waves = pick.shape[0]
    members = waves // GROUPS
    lane = lax.broadcasted_iota(I32, (2 * lat_dev * SUB, LANES), 1)
    open_tile = None
    for g in range(GROUPS):
        high, top = yhi[g], thi[g]
        z = dot(
            jnp.concatenate([high, high, ylo[g]], axis=1),
            jnp.concatenate([top, tlo[g], top], axis=0),
        )
        re = z[:, :LANES].reshape(lat_dev, 1, SUB, LANES)
        im = z[:, LANES:].reshape(lat_dev, 1, SUB, LANES)
        both = jnp.concatenate([re, im], axis=1).reshape(lat_dev * 2 * SUB, LANES)
        tile, offset = divmod(g * members, LANES)
        past = offset + members - LANES
        mine = jnp.where(lane >= offset, both, 0.0) if past > 0 else both
        open_tile = mine if open_tile is None else open_tile + mine
        if past >= 0:
            hi, lo = split(open_tile.T)
            zt[tile * LANES : (tile + 1) * LANES, :] = hi
            zt[waves + tile * LANES : waves + (tile + 1) * LANES, :] = lo
            open_tile = jnp.where(lane < past, both, 0.0) if past > 0 else None

    chunks = zt.shape[1] // LANES
    tall = LANES
    sends = []
    for j0 in range(0, waves, tall):
        sel = pick[j0 : j0 + tall, :]
        res = dot(jnp.concatenate([sel, sel], axis=1), zt[...])
        for jt in range(tall // SUB):
            for c in range(chunks):
                start = (j0 + jt * SUB) * chunks + c
                out[pl.ds(start, SUB, stride=chunks), :] = res[
                    jt * SUB : (jt + 1) * SUB, c * LANES : (c + 1) * LANES
                ]
        span = pl.ds(j0 * chunks, tall * chunks)
        sends.append(
            pltpu.make_async_copy(out.at[span], out_hbm.at[span], sems.at[11 + j0 // tall])
        )
        sends[-1].start()
    for copy in sends:
        copy.wait()


def grid_to_waves(recv, gain, thi, tlo, pick):
    lat_dev, ch_dev, lon_count = gain.shape
    waves = pick.shape[0]
    groups, capacity = recv.shape[0], recv.shape[1] - SUB
    cells = lat_dev * lon_count // LANES
    rows = lat_dev * ch_dev
    return pl.pallas_call(
        grid_kernel,
        out_shape=jax.ShapeDtypeStruct((waves * 2 * rows // LANES, LANES), F32),
        in_specs=[pl.BlockSpec(memory_space=pltpu.HBM)] * 5,
        out_specs=pl.BlockSpec(memory_space=pltpu.HBM),
        scratch_shapes=[pltpu.VMEM((cells, ch_dev, LANES), F32) for _ in range(STREAMS)]
        + [
            pltpu.VMEM((groups, capacity, LANES), F32),
            pltpu.VMEM((groups, SUB, LANES), F32),
            pltpu.VMEM(gain.shape, F32),
            pltpu.VMEM(thi.shape, BF16),
            pltpu.VMEM(tlo.shape, BF16),
            pltpu.VMEM(pick.shape, BF16),
            pltpu.VMEM((groups, LANES), I32),
            pltpu.SMEM((groups, LANES), I32),
            pltpu.VMEM((groups * SUB, 2 * LANES), F32),
            pltpu.VMEM((groups * SUB, 2 * LANES), F32),
            pltpu.VMEM((GROUPS, rows, thi.shape[1]), BF16),
            pltpu.VMEM((GROUPS, rows, thi.shape[1]), BF16),
            pltpu.VMEM((2 * waves, 2 * rows), BF16),
            pltpu.VMEM((waves * 2 * rows // LANES, LANES), F32),
            pltpu.SemaphoreType.DMA((11 + waves // LANES,)),
        ],
        compiler_params=pltpu.CompilerParams(vmem_limit_bytes=52 * MIB),
        name="grid_to_waves",
    )(recv, gain, thi, tlo, pick)


def prepare_kernel(lat_dev, band_ref, table_ref, hi_ref, lo_ref):
    grid_count = band_ref.shape[0]
    chunks = lat_dev // SUB
    full = LANES // grid_count
    assert chunks == full + 1
    half = 2 * SUB

    def body(c, carry):
        starts = [
            pl.multiple_of(band_ref[g] * lat_dev + c * SUB, SUB) for g in range(grid_count)
        ]
        for t in range(table_ref.shape[2] // LANES):
            lanes = pl.ds(t * LANES, LANES)
            for g0 in range(0, grid_count, half):
                turned = []
                for g1 in range(g0, g0 + half, SUB):
                    tiles = [
                        table_ref[0, pl.ds(starts[g], SUB), lanes] for g in range(g1, g1 + SUB)
                    ]
                    turned.append(jnp.swapaxes(jnp.stack(tiles), 0, 1))
                for k in range(SUB):
                    hi, lo = split(jnp.concatenate([x[k] for x in turned], axis=0))
                    start = jnp.where(
                        c < full, k * LANES + c * grid_count, full * SUB * grid_count + k * grid_count
                    )
                    start = pl.multiple_of(start + g0, half)
                    hi_ref[0, pl.ds(start, half), lanes] = hi
                    lo_ref[0, pl.ds(start, half), lanes] = lo
        return carry

    lax.fori_loop(0, chunks, body, 0)


def prepare_table(legendre, band_of, lat_dev):
    slot_count, lat_total, total_count = legendre.shape
    block = pl.BlockSpec((1, lat_total, total_count), lambda s: (s, 0, 0))
    return pl.pallas_call(
        functools.partial(prepare_kernel, lat_dev),
        grid=(slot_count,),
        out_shape=[jax.ShapeDtypeStruct(legendre.shape, BF16)] * 2,
        in_specs=[pl.BlockSpec(memory_space=pltpu.SMEM), block],
        out_specs=[block, block],
        compiler_params=pltpu.CompilerParams(vmem_limit_bytes=56 * MIB),
        cost_estimate=pl.CostEstimate(
            flops=4 * legendre.size, bytes_accessed=8 * legendre.size, transcendentals=0
        ),
        name="prepare_table",
    )(band_of, legendre)


def legendre_kernel(geo, x_hbm, lhi_hbm, llo_hbm, out_hbm, x_ref, lhi, llo, out, sems):
    grid_count, lev_count, slot_count, chunks = geo
    full = LANES // grid_count
    wide = 2 * SUB
    first = pltpu.make_async_copy(x_hbm, x_ref, sems.at[0])
    first.start()

    def loads(slot):
        return [
            pltpu.make_async_copy(src.at[slot], dst.at[slot], sems.at[1 + 2 * slot + i])
            for i, (src, dst) in enumerate(((lhi_hbm, lhi), (llo_hbm, llo)))
        ]

    for slot in range(AHEAD):
        for copy in loads(slot):
            copy.start()
    first.wait()

    def store(slot):
        return pltpu.make_async_copy(
            out.at[slot], out_hbm.at[slot], sems.at[1 + 2 * slot_count + slot]
        )

    def body(slot, carry):
        lhs = []
        for lev in range(lev_count):
            pieces = []
            for c in range(chunks):
                start = (lev * slot_count + slot) * chunks + c
                pieces.append(
                    x_ref[pl.ds(start, grid_count, stride=lev_count * slot_count * chunks), :]
                )
            lhs.append(jnp.concatenate(pieces, axis=0).T)
        for copy in loads(slot):
            copy.wait()

        @pl.when(slot + AHEAD < slot_count)
        def _():
            for copy in loads(slot + AHEAD):
                copy.start()

        steps = range(LANES // wide)
        cut = full * grid_count
        main = [
            jnp.concatenate([m[k * wide : (k + 1) * wide, :cut] for m in lhs], axis=0) for k in steps
        ]
        rest = [
            jnp.concatenate([m[k * wide : (k + 1) * wide, cut:] for m in lhs], axis=0) for k in steps
        ]
        hi, lo = split(jnp.concatenate(main + rest, axis=1))
        both = jnp.concatenate([hi, lo], axis=0)
        prod = jnp.dot(both, lhi[slot], preferred_element_type=F32)
        tail = jnp.dot(hi, llo[slot], preferred_element_type=F32)
        total = prod[: hi.shape[0]] + (prod[hi.shape[0] :] + tail)
        for lev in range(lev_count):
            re = total[lev * wide : lev * wide + SUB]
            im = total[lev * wide + SUB : (lev + 1) * wide]
            out[slot, lev * SUB : (lev + 1) * SUB] = jnp.stack([re, im], axis=1)
        store(slot).start()
        return carry

    lax.fori_loop(0, slot_count, body, 0)
    for slot in range(slot_count):
        store(slot).wait()


def legendre_step(waves, lhi, llo, grid_count, lev_count):
    slot_count, lat_total, total_count = lhi.shape
    chunks = waves.shape[0] // (grid_count * lev_count * slot_count)
    geo = (grid_count, lev_count, slot_count, chunks)
    out_shape = (slot_count, lev_count * SUB, 2, total_count)
    return pl.pallas_call(
        functools.partial(legendre_kernel, geo),
        out_shape=jax.ShapeDtypeStruct(out_shape, F32),
        in_specs=[pl.BlockSpec(memory_space=pltpu.HBM)] * 3,
        out_specs=pl.BlockSpec(memory_space=pltpu.HBM),
        scratch_shapes=[
            pltpu.VMEM(waves.shape, F32),
            pltpu.VMEM(lhi.shape, BF16),
            pltpu.VMEM(llo.shape, BF16),
            pltpu.VMEM(out_shape, F32),
            pltpu.SemaphoreType.DMA((1 + 3 * slot_count,)),
        ],
        compiler_params=pltpu.CompilerParams(vmem_limit_bytes=50 * MIB),
        name="legendre_step",
    )(waves, lhi, llo)


def shards(trajectory, legendre, obs_cell, obs_count, departure, obs_weight, band_of, m_order):
    grid_count = lax.axis_size("grid")
    lev_count = lax.axis_size("lev")
    ch_dev, lat_dev, lon_count = trajectory.shape
    slot_count, lat_total, total_count = legendre.shape
    wave_total = m_order.shape[0]
    cells_per_dev = lat_dev * lon_count // LANES

    sent = pack(obs_count, departure, obs_weight, obs_cell, cells_per_dev)
    recv = lax.all_to_all(sent, "grid", split_axis=0, concat_axis=0, tiled=True)

    gain = jnp.swapaxes(1.0 + 0.5 * jnp.tanh(trajectory), 0, 1)
    thi, tlo = split_np(wave_table(wave_total, lon_count))
    cols = wave_columns(wave_total).reshape(1, -1)
    pick = (m_order[:, None] == cols).astype(BF16)

    waves = grid_to_waves(recv, gain, jnp.asarray(thi), jnp.asarray(tlo), pick)
    outgoing = waves.reshape(grid_count * lev_count, 1, -1)
    incoming = lax.all_to_all(
        outgoing, ("grid", "lev"), split_axis=0, concat_axis=0, tiled=True
    )

    lhi, llo = prepare_table(legendre, band_of, lat_dev)
    return legendre_step(
        incoming.reshape(-1, LANES), lhi, llo, grid_count, lev_count
    )


def solution(mesh):
    placed = (
        P("lev", "grid", None),
        P(("grid", "lev"), None, None),
        P("grid"),
        P("grid"),
        P("grid", None),
        P("lev", "grid"),
        P(),
        P(),
    )
    return jax.shard_map(
        shards,
        mesh=mesh,
        in_specs=placed,
        out_specs=P(("grid", "lev"), None, None, None),
        check_vma=False,
    )
```

```python
import functools
import math

import jax
import jax.numpy as jnp
import numpy as np
from jax import lax
from jax.experimental import pallas as pl
from jax.experimental.pallas import tpu as pltpu
from jax.sharding import PartitionSpec as P

LANES = 128
SUB = 8
RADIX = 16
GROUPS = RADIX // 2
MIB = 1 << 20
F32 = jnp.float32
BF16 = jnp.bfloat16
I32 = jnp.int32


def wave_columns(wave_total):
    per_residue = wave_total // RADIX
    cols = np.zeros((GROUPS, 2 * per_residue), np.int32)
    for g in range(GROUPS):
        first, second = g, (RADIX - g if g else RADIX // 2)
        turns = RADIX * np.arange(per_residue)
        cols[g, :per_residue] = first + turns
        cols[g, per_residue : 2 * per_residue] = second + turns
    return cols


def wave_table(wave_total, lon_count):
    width = lon_count // RADIX
    cols = wave_columns(wave_total)
    per_residue = wave_total // RADIX
    fine = np.arange(width, dtype=np.int64)
    out = np.zeros((GROUPS, 2, width, 2, LANES), np.float64)
    for g in range(GROUPS):
        for i in range(2 * per_residue):
            m = int(cols[g, i])
            lane = (g * 2 * per_residue + i) % LANES
            angle = 2.0 * math.pi / lon_count * ((m * fine) % lon_count)
            factor = 1.0 if m == 0 else 2.0
            cos, sin = factor * np.cos(angle), factor * np.sin(angle)
            second = i >= per_residue
            if g == 0:
                part = 1 if second else 0
                out[g, part, :, 0, lane] = cos
                out[g, part, :, 1, lane] = -sin
            else:
                sign = -1.0 if second else 1.0
                out[g, 0, :, 0, lane] = cos
                out[g, 1, :, 0, lane] = sign * sin
                out[g, 0, :, 1, lane] = -sin
                out[g, 1, :, 1, lane] = sign * cos
    return out.reshape(GROUPS, 2 * width, 2 * LANES).astype(np.float32)


def split_np(table):
    high = table.astype(jnp.bfloat16)
    low = (table - high.astype(np.float32)).astype(jnp.bfloat16)
    return high, low


def split(x):
    high = x.astype(BF16)
    return high, (x - high.astype(F32)).astype(BF16)


def real_fft(xs):
    n = len(xs)
    if n == 2:
        return [(xs[0] + xs[1], None), (xs[0] - xs[1], None)]
    even, odd = real_fft(xs[0::2]), real_fft(xs[1::2])
    out = [None] * (n // 2 + 1)
    for k in range(n // 4 + 1):
        er, ei = even[k]
        orr, oi = odd[k]
        if k == 0:
            out[0] = (er + orr, None)
            out[n // 2] = (er - orr, None)
        elif 4 * k == n:
            out[k] = (er, -orr)
        else:
            c, s = math.cos(2 * math.pi * k / n), math.sin(2 * math.pi * k / n)
            if 8 * k == n:
                tr, ti = (orr + oi) * c, (oi - orr) * c
            else:
                tr, ti = orr * c + oi * s, oi * c - orr * s
            out[k] = (er + tr, ei + ti)
            out[n // 2 - k] = (er - tr, ti - ei)
    return out


def pack_kernel(
    capacity, cells_per_dev, count_hbm, dep_hbm, weight_hbm, cell_hbm, out_hbm,
    counts, weights, cells_v, out, sems,
):
    groups = out.shape[0]
    small = [
        pltpu.make_async_copy(src, dst, sems.at[i])
        for i, (src, dst) in enumerate(
            ((count_hbm, counts), (weight_hbm, weights), (cell_hbm, cells_v))
        )
    ]
    for copy in small:
        copy.start()
    parts = 4
    each = groups // parts
    large = [
        pltpu.make_async_copy(
            dep_hbm.at[pl.ds(i * each, each)],
            out.at[pl.ds(i * each, each), pl.ds(0, capacity)],
            sems.at[3 + i],
        )
        for i in range(parts)
    ]
    for copy in large:
        copy.start()
    for copy in small:
        copy.wait()
    lane = lax.broadcasted_iota(I32, (SUB, LANES), 1)
    for q in range(groups):
        tile = q // 2
        weight = weights[:, tile * LANES : (tile + 1) * LANES]
        cells = jnp.broadcast_to(cells_v[tile : tile + 1, :], (SUB, LANES))
        cells = (cells - q * cells_per_dev).astype(F32)
        if q % 2:
            weight = pltpu.roll(weight, capacity, 1)
        else:
            cells = pltpu.roll(cells, capacity, 1)
        live = jnp.where(lane < counts[q], 1.0, 0.0)
        out[q, capacity:, :] = jnp.where(lane < capacity, weight * live, cells)
    sends = []
    for i in range(parts):
        large[i].wait()
        span = pl.ds(i * each, each)
        sends.append(
            pltpu.make_async_copy(out.at[span], out_hbm.at[span], sems.at[3 + parts + i])
        )
        sends[-1].start()
    for copy in sends:
        copy.wait()


def pack(obs_count, departure, obs_weight, obs_cell, cells_per_dev):
    groups = obs_count.shape[0]
    slots = departure.shape[0]
    capacity = slots // groups
    assert 2 * capacity == LANES and obs_weight.shape[0] == SUB
    cell_rows = obs_cell.reshape(slots // LANES, LANES)
    out_shape = (groups, capacity + SUB, LANES)
    return pl.pallas_call(
        functools.partial(pack_kernel, capacity, cells_per_dev),
        out_shape=jax.ShapeDtypeStruct(out_shape, F32),
        in_specs=[pl.BlockSpec(memory_space=pltpu.HBM)] * 4,
        out_specs=pl.BlockSpec(memory_space=pltpu.HBM),
        scratch_shapes=[
            pltpu.SMEM(obs_count.shape, I32),
            pltpu.VMEM(obs_weight.shape, F32),
            pltpu.VMEM(cell_rows.shape, I32),
            pltpu.VMEM(out_shape, F32),
            pltpu.SemaphoreType.DMA((11,)),
        ],
        compiler_params=pltpu.CompilerParams(vmem_limit_bytes=60 * MIB),
        name="pack",
    )(obs_count, departure.reshape(groups, capacity, LANES), obs_weight, cell_rows)


STREAMS = 4
AHEAD = 5


def grid_kernel(
    recv, gain_hbm, thi_hbm, tlo_hbm, pick_hbm, out_hbm, *scratch
):
    acc = scratch[:STREAMS]
    gain, thi, tlo, pick, cells_v, cells_s, wide_a, wide_b, yhi, ylo, zt, out, sems = scratch[
        STREAMS:
    ]
    groups, rows_in, _ = recv.shape
    capacity = rows_in - SUB
    lat_dev = gain.shape[0]
    blocks = gain.shape[2] // LANES
    half = lat_dev // 2
    loads = [
        pltpu.make_async_copy(src, dst, sems.at[1 + i])
        for i, (src, dst) in enumerate(
            (
                (gain_hbm.at[pl.ds(0, half)], gain.at[pl.ds(0, half)]),
                (gain_hbm.at[pl.ds(half, half)], gain.at[pl.ds(half, half)]),
                (thi_hbm, thi),
                (tlo_hbm, tlo),
                (pick_hbm, pick),
            )
        )
    ]
    for copy in loads:
        copy.start()

    cells_v[...] = recv[:, capacity, :].astype(I32)
    cell_copy = pltpu.make_async_copy(cells_v, cells_s, sems.at[0])
    cell_copy.start()

    def clear(i, carry):
        for a in acc:
            a[pl.ds(i * SUB, SUB)] = jnp.zeros((SUB, SUB, LANES), F32)
        return carry

    lax.fori_loop(0, acc[0].shape[0] // SUB, clear, 0)


    rows = groups * SUB
    weight = recv[:, capacity:, :].reshape(rows, LANES)
    lane = lax.broadcasted_iota(I32, (rows, LANES), 1)
    whi, wlo = split(weight)
    both = jnp.where(
        lane < capacity, whi.astype(F32), pltpu.roll(wlo.astype(F32), capacity, 1)
    ).astype(BF16)
    row = lax.broadcasted_iota(I32, (LANES, 2 * LANES), 0) % capacity
    col = lax.broadcasted_iota(I32, (LANES, 2 * LANES), 1) // LANES
    offset = row - col

    def widen(ref, k0):
        ones = jnp.where(offset == k0, 1.0, 0.0).astype(BF16)
        ref[...] = jnp.dot(both, ones, preferred_element_type=F32)

    def add_slots(ref, k0):
        per = STREAMS // 2
        for s0 in range(0, groups, per):
            slots = [(s0 + t // 2, t % 2) for t in range(STREAMS)]
            cells = [cells_s[s, capacity + k0 + kk] for s, kk in slots]
            old = [acc[t][cells[t]] for t in range(STREAMS)]
            new = []
            for t, (s, kk) in enumerate(slots):
                weights = ref[s * SUB : (s + 1) * SUB, kk * LANES : (kk + 1) * LANES]
                new.append(old[t] + weights * recv[s, pl.ds(k0 + kk, 1), :])
            for t in range(STREAMS):
                acc[t][cells[t]] = new[t]

    widen(wide_a, 0)
    cell_copy.wait()

    def scatter(i, carry):
        k0 = 4 * i
        widen(wide_b, k0 + 2)
        add_slots(wide_a, k0)
        widen(wide_a, k0 + 4)
        add_slots(wide_b, k0 + 2)
        return carry

    lax.fori_loop(0, capacity // 4, scatter, 0)
    for copy in loads[:2]:
        copy.wait()

    width = blocks // RADIX * LANES
    pair = 2

    def transform(i, carry):
        r0 = i * pair
        for h in range(blocks // RADIX):
            xs = []
            for a in range(RADIX):
                b = a * (blocks // RADIX) + h
                parts = []
                for r in range(pair):
                    cell = (r0 + r) * blocks + b
                    total = acc[0][cell]
                    for t in range(1, STREAMS):
                        total = total + acc[t][cell]
                    parts.append(total * gain[r0 + r, :, b * LANES : (b + 1) * LANES])
                xs.append(jnp.concatenate(parts, axis=0))
            ys = real_fft(xs)
            rows = pl.ds(pl.multiple_of(r0 * SUB, pair * SUB), pair * SUB)
            for g in range(GROUPS):
                re, im = ys[g] if g else (ys[0][0], ys[RADIX // 2][0])
                for part, value in enumerate((re, im)):
                    lanes = pl.ds(part * width + h * LANES, LANES)
                    hi, lo = split(value)
                    yhi[g, rows, lanes] = hi
                    ylo[g, rows, lanes] = lo
        return carry

    lax.fori_loop(0, lat_dev // pair, transform, 0)
    for copy in loads[2:]:
        copy.wait()

    def dot(a, b):
        return jnp.dot(a, b, preferred_element_type=F32)

    waves = pick.shape[0]
    members = waves // GROUPS
    lane = lax.broadcasted_iota(I32, (2 * lat_dev * SUB, LANES), 1)
    open_tile = None
    for g in range(GROUPS):
        high, top = yhi[g], thi[g]
        z = dot(
            jnp.concatenate([high, high, ylo[g]], axis=1),
            jnp.concatenate([top, tlo[g], top], axis=0),
        )
        re = z[:, :LANES].reshape(lat_dev, 1, SUB, LANES)
        im = z[:, LANES:].reshape(lat_dev, 1, SUB, LANES)
        both = jnp.concatenate([re, im], axis=1).reshape(lat_dev * 2 * SUB, LANES)
        tile, offset = divmod(g * members, LANES)
        past = offset + members - LANES
        mine = jnp.where(lane >= offset, both, 0.0) if past > 0 else both
        open_tile = mine if open_tile is None else open_tile + mine
        if past >= 0:
            hi, lo = split(open_tile.T)
            zt[tile * LANES : (tile + 1) * LANES, :] = hi
            zt[waves + tile * LANES : waves + (tile + 1) * LANES, :] = lo
            open_tile = jnp.where(lane < past, both, 0.0) if past > 0 else None

    chunks = zt.shape[1] // LANES
    tall = LANES
    sends = []
    for j0 in range(0, waves, tall):
        sel = pick[j0 : j0 + tall, :]
        res = dot(jnp.concatenate([sel, sel], axis=1), zt[...])
        for jt in range(tall // SUB):
            for c in range(chunks):
                start = (j0 + jt * SUB) * chunks + c
                out[pl.ds(start, SUB, stride=chunks), :] = res[
                    jt * SUB : (jt + 1) * SUB, c * LANES : (c + 1) * LANES
                ]
        span = pl.ds(j0 * chunks, tall * chunks)
        sends.append(
            pltpu.make_async_copy(out.at[span], out_hbm.at[span], sems.at[6 + j0 // tall])
        )
        sends[-1].start()
    for copy in sends:
        copy.wait()


def grid_to_waves(recv, gain, thi, tlo, pick):
    lat_dev, ch_dev, lon_count = gain.shape
    waves = pick.shape[0]
    groups, capacity = recv.shape[0], recv.shape[1] - SUB
    cells = lat_dev * lon_count // LANES
    rows = lat_dev * ch_dev
    return pl.pallas_call(
        grid_kernel,
        out_shape=jax.ShapeDtypeStruct((waves * 2 * rows // LANES, LANES), F32),
        in_specs=[pl.BlockSpec(memory_space=pltpu.VMEM)]
        + [pl.BlockSpec(memory_space=pltpu.HBM)] * 4,
        out_specs=pl.BlockSpec(memory_space=pltpu.HBM),
        scratch_shapes=[pltpu.VMEM((cells, ch_dev, LANES), F32) for _ in range(STREAMS)]
        + [
            pltpu.VMEM(gain.shape, F32),
            pltpu.VMEM(thi.shape, BF16),
            pltpu.VMEM(tlo.shape, BF16),
            pltpu.VMEM(pick.shape, BF16),
            pltpu.VMEM((groups, LANES), I32),
            pltpu.SMEM((groups, LANES), I32),
            pltpu.VMEM((groups * SUB, 2 * LANES), F32),
            pltpu.VMEM((groups * SUB, 2 * LANES), F32),
            pltpu.VMEM((GROUPS, rows, thi.shape[1]), BF16),
            pltpu.VMEM((GROUPS, rows, thi.shape[1]), BF16),
            pltpu.VMEM((2 * waves, 2 * rows), BF16),
            pltpu.VMEM((waves * 2 * rows // LANES, LANES), F32),
            pltpu.SemaphoreType.DMA((6 + waves // LANES,)),
        ],
        compiler_params=pltpu.CompilerParams(vmem_limit_bytes=52 * MIB),
        name="grid_to_waves",
    )(recv, gain, thi, tlo, pick)


def prepare_kernel(lat_dev, band_ref, table_ref, hi_ref, lo_ref):
    grid_count = band_ref.shape[0]
    chunks = lat_dev // SUB
    full = LANES // grid_count
    assert chunks == full + 1
    half = 2 * SUB

    def body(c, carry):
        starts = [
            pl.multiple_of(band_ref[g] * lat_dev + c * SUB, SUB) for g in range(grid_count)
        ]
        for t in range(table_ref.shape[2] // LANES):
            lanes = pl.ds(t * LANES, LANES)
            for g0 in range(0, grid_count, half):
                turned = []
                for g1 in range(g0, g0 + half, SUB):
                    tiles = [
                        table_ref[0, pl.ds(starts[g], SUB), lanes] for g in range(g1, g1 + SUB)
                    ]
                    turned.append(jnp.swapaxes(jnp.stack(tiles), 0, 1))
                for k in range(SUB):
                    hi, lo = split(jnp.concatenate([x[k] for x in turned], axis=0))
                    start = jnp.where(
                        c < full, k * LANES + c * grid_count, full * SUB * grid_count + k * grid_count
                    )
                    start = pl.multiple_of(start + g0, half)
                    hi_ref[0, pl.ds(start, half), lanes] = hi
                    lo_ref[0, pl.ds(start, half), lanes] = lo
        return carry

    lax.fori_loop(0, chunks, body, 0)


def prepare_table(legendre, band_of, lat_dev):
    slot_count, lat_total, total_count = legendre.shape
    block = pl.BlockSpec((1, lat_total, total_count), lambda s: (s, 0, 0))
    return pl.pallas_call(
        functools.partial(prepare_kernel, lat_dev),
        grid=(slot_count,),
        out_shape=[jax.ShapeDtypeStruct(legendre.shape, BF16)] * 2,
        in_specs=[pl.BlockSpec(memory_space=pltpu.SMEM), block],
        out_specs=[block, block],
        compiler_params=pltpu.CompilerParams(vmem_limit_bytes=56 * MIB),
        cost_estimate=pl.CostEstimate(
            flops=4 * legendre.size, bytes_accessed=8 * legendre.size, transcendentals=0
        ),
        name="prepare_table",
    )(band_of, legendre)


def legendre_kernel(geo, x_ref, lhi_hbm, llo_hbm, out_hbm, lhi, llo, out, sems):
    grid_count, lev_count, slot_count, chunks = geo
    full = LANES // grid_count
    wide = 2 * SUB
    def loads(slot):
        return [
            pltpu.make_async_copy(src.at[slot], dst.at[slot], sems.at[2 * slot + i])
            for i, (src, dst) in enumerate(((lhi_hbm, lhi), (llo_hbm, llo)))
        ]

    for slot in range(AHEAD):
        for copy in loads(slot):
            copy.start()

    def store(slot):
        return pltpu.make_async_copy(
            out.at[slot], out_hbm.at[slot], sems.at[2 * slot_count + slot]
        )

    def body(slot, carry):
        lhs = []
        for lev in range(lev_count):
            pieces = []
            for c in range(chunks):
                start = (lev * slot_count + slot) * chunks + c
                pieces.append(
                    x_ref[pl.ds(start, grid_count, stride=lev_count * slot_count * chunks), :]
                )
            lhs.append(jnp.concatenate(pieces, axis=0).T)
        for copy in loads(slot):
            copy.wait()

        @pl.when(slot + AHEAD < slot_count)
        def _():
            for copy in loads(slot + AHEAD):
                copy.start()

        steps = range(LANES // wide)
        cut = full * grid_count
        main = [
            jnp.concatenate([m[k * wide : (k + 1) * wide, :cut] for m in lhs], axis=0) for k in steps
        ]
        rest = [
            jnp.concatenate([m[k * wide : (k + 1) * wide, cut:] for m in lhs], axis=0) for k in steps
        ]
        hi, lo = split(jnp.concatenate(main + rest, axis=1))
        both = jnp.concatenate([hi, lo], axis=0)
        prod = jnp.dot(both, lhi[slot], preferred_element_type=F32)
        tail = jnp.dot(hi, llo[slot], preferred_element_type=F32)
        total = prod[: hi.shape[0]] + (prod[hi.shape[0] :] + tail)
        for lev in range(lev_count):
            re = total[lev * wide : lev * wide + SUB]
            im = total[lev * wide + SUB : (lev + 1) * wide]
            out[slot, lev * SUB : (lev + 1) * SUB] = jnp.stack([re, im], axis=1)
        store(slot).start()
        return carry

    lax.fori_loop(0, slot_count, body, 0)
    for slot in range(slot_count):
        store(slot).wait()


def legendre_step(waves, lhi, llo, grid_count, lev_count):
    slot_count, lat_total, total_count = lhi.shape
    chunks = waves.shape[0] // (grid_count * lev_count * slot_count)
    geo = (grid_count, lev_count, slot_count, chunks)
    out_shape = (slot_count, lev_count * SUB, 2, total_count)
    return pl.pallas_call(
        functools.partial(legendre_kernel, geo),
        out_shape=jax.ShapeDtypeStruct(out_shape, F32),
        in_specs=[pl.BlockSpec(memory_space=pltpu.VMEM)]
        + [pl.BlockSpec(memory_space=pltpu.HBM)] * 2,
        out_specs=pl.BlockSpec(memory_space=pltpu.HBM),
        scratch_shapes=[
            pltpu.VMEM(lhi.shape, BF16),
            pltpu.VMEM(llo.shape, BF16),
            pltpu.VMEM(out_shape, F32),
            pltpu.SemaphoreType.DMA((3 * slot_count,)),
        ],
        compiler_params=pltpu.CompilerParams(vmem_limit_bytes=50 * MIB),
        name="legendre_step",
    )(waves, lhi, llo)


def shards(trajectory, legendre, obs_cell, obs_count, departure, obs_weight, band_of, m_order):
    grid_count = lax.axis_size("grid")
    lev_count = lax.axis_size("lev")
    ch_dev, lat_dev, lon_count = trajectory.shape
    slot_count, lat_total, total_count = legendre.shape
    wave_total = m_order.shape[0]
    cells_per_dev = lat_dev * lon_count // LANES

    sent = pack(obs_count, departure, obs_weight, obs_cell, cells_per_dev)
    recv = lax.all_to_all(sent, "grid", split_axis=0, concat_axis=0, tiled=True)

    gain = jnp.swapaxes(1.0 + 0.5 * jnp.tanh(trajectory), 0, 1)
    thi, tlo = split_np(wave_table(wave_total, lon_count))
    cols = wave_columns(wave_total).reshape(1, -1)
    pick = (m_order[:, None] == cols).astype(BF16)

    waves = grid_to_waves(recv, gain, jnp.asarray(thi), jnp.asarray(tlo), pick)
    outgoing = waves.reshape(grid_count * lev_count, 1, -1)
    incoming = lax.all_to_all(
        outgoing, ("grid", "lev"), split_axis=0, concat_axis=0, tiled=True
    )

    lhi, llo = prepare_table(legendre, band_of, lat_dev)
    return legendre_step(
        incoming.reshape(-1, LANES), lhi, llo, grid_count, lev_count
    )


def solution(mesh):
    placed = (
        P("lev", "grid", None),
        P(("grid", "lev"), None, None),
        P("grid"),
        P("grid"),
        P("grid", None),
        P("lev", "grid"),
        P(),
        P(),
    )
    return jax.shard_map(
        shards,
        mesh=mesh,
        in_specs=placed,
        out_specs=P(("grid", "lev"), None, None, None),
        check_vma=False,
    )
```

```python
import functools
import math

import jax
import jax.numpy as jnp
import numpy as np
from jax import lax
from jax.experimental import pallas as pl
from jax.experimental.pallas import tpu as pltpu
from jax.sharding import PartitionSpec as P

LANES = 128
SUB = 8
RADIX = 16
GROUPS = RADIX // 2
MIB = 1 << 20
F32 = jnp.float32
BF16 = jnp.bfloat16
I32 = jnp.int32


def wave_columns(wave_total):
    per_residue = wave_total // RADIX
    cols = np.zeros((GROUPS, 2 * per_residue), np.int32)
    for g in range(GROUPS):
        first, second = g, (RADIX - g if g else RADIX // 2)
        turns = RADIX * np.arange(per_residue)
        cols[g, :per_residue] = first + turns
        cols[g, per_residue : 2 * per_residue] = second + turns
    return cols


def wave_table(wave_total, lon_count):
    width = lon_count // RADIX
    cols = wave_columns(wave_total)
    per_residue = wave_total // RADIX
    fine = np.arange(width, dtype=np.int64)
    out = np.zeros((GROUPS, 2, width, 2, LANES), np.float64)
    for g in range(GROUPS):
        for i in range(2 * per_residue):
            m = int(cols[g, i])
            lane = (g * 2 * per_residue + i) % LANES
            angle = 2.0 * math.pi / lon_count * ((m * fine) % lon_count)
            factor = 1.0 if m == 0 else 2.0
            cos, sin = factor * np.cos(angle), factor * np.sin(angle)
            second = i >= per_residue
            if g == 0:
                part = 1 if second else 0
                out[g, part, :, 0, lane] = cos
                out[g, part, :, 1, lane] = -sin
            else:
                sign = -1.0 if second else 1.0
                out[g, 0, :, 0, lane] = cos
                out[g, 1, :, 0, lane] = sign * sin
                out[g, 0, :, 1, lane] = -sin
                out[g, 1, :, 1, lane] = sign * cos
    return out.reshape(GROUPS, 2 * width, 2 * LANES).astype(np.float32)


def split_np(table):
    high = table.astype(jnp.bfloat16)
    low = (table - high.astype(np.float32)).astype(jnp.bfloat16)
    return high, low


def split(x):
    high = x.astype(BF16)
    return high, (x - high.astype(F32)).astype(BF16)


def real_fft(xs):
    n = len(xs)
    if n == 2:
        return [(xs[0] + xs[1], None), (xs[0] - xs[1], None)]
    even, odd = real_fft(xs[0::2]), real_fft(xs[1::2])
    out = [None] * (n // 2 + 1)
    for k in range(n // 4 + 1):
        er, ei = even[k]
        orr, oi = odd[k]
        if k == 0:
            out[0] = (er + orr, None)
            out[n // 2] = (er - orr, None)
        elif 4 * k == n:
            out[k] = (er, -orr)
        else:
            c, s = math.cos(2 * math.pi * k / n), math.sin(2 * math.pi * k / n)
            if 8 * k == n:
                tr, ti = (orr + oi) * c, (oi - orr) * c
            else:
                tr, ti = orr * c + oi * s, oi * c - orr * s
            out[k] = (er + tr, ei + ti)
            out[n // 2 - k] = (er - tr, ti - ei)
    return out


def pack_kernel(
    capacity, cells_per_dev, count_hbm, dep_hbm, weight_hbm, cell_hbm, out_hbm,
    counts, weights, cells_v, out, sems,
):
    groups = out.shape[0]
    small = [
        pltpu.make_async_copy(src, dst, sems.at[i])
        for i, (src, dst) in enumerate(
            ((count_hbm, counts), (weight_hbm, weights), (cell_hbm, cells_v))
        )
    ]
    for copy in small:
        copy.start()
    parts = 4
    each = groups // parts
    large = [
        pltpu.make_async_copy(
            dep_hbm.at[pl.ds(i * each, each)],
            out.at[pl.ds(i * each, each), pl.ds(0, capacity)],
            sems.at[3 + i],
        )
        for i in range(parts)
    ]
    for copy in large:
        copy.start()
    for copy in small:
        copy.wait()
    lane = lax.broadcasted_iota(I32, (SUB, LANES), 1)
    for q in range(groups):
        tile = q // 2
        weight = weights[:, tile * LANES : (tile + 1) * LANES]
        cells = jnp.broadcast_to(cells_v[tile : tile + 1, :], (SUB, LANES))
        cells = (cells - q * cells_per_dev).astype(F32)
        if q % 2:
            weight = pltpu.roll(weight, capacity, 1)
        else:
            cells = pltpu.roll(cells, capacity, 1)
        live = jnp.where(lane < counts[q], 1.0, 0.0)
        out[q, capacity:, :] = jnp.where(lane < capacity, weight * live, cells)
    sends = []
    for i in range(parts):
        large[i].wait()
        span = pl.ds(i * each, each)
        sends.append(
            pltpu.make_async_copy(out.at[span], out_hbm.at[span], sems.at[3 + parts + i])
        )
        sends[-1].start()
    for copy in sends:
        copy.wait()


def pack(obs_count, departure, obs_weight, obs_cell, cells_per_dev):
    groups = obs_count.shape[0]
    slots = departure.shape[0]
    capacity = slots // groups
    assert 2 * capacity == LANES and obs_weight.shape[0] == SUB
    cell_rows = obs_cell.reshape(slots // LANES, LANES)
    out_shape = (groups, capacity + SUB, LANES)
    return pl.pallas_call(
        functools.partial(pack_kernel, capacity, cells_per_dev),
        out_shape=jax.ShapeDtypeStruct(out_shape, F32),
        in_specs=[pl.BlockSpec(memory_space=pltpu.HBM)] * 4,
        out_specs=pl.BlockSpec(memory_space=pltpu.HBM),
        scratch_shapes=[
            pltpu.SMEM(obs_count.shape, I32),
            pltpu.VMEM(obs_weight.shape, F32),
            pltpu.VMEM(cell_rows.shape, I32),
            pltpu.VMEM(out_shape, F32),
            pltpu.SemaphoreType.DMA((11,)),
        ],
        compiler_params=pltpu.CompilerParams(vmem_limit_bytes=60 * MIB),
        name="pack",
    )(obs_count, departure.reshape(groups, capacity, LANES), obs_weight, cell_rows)


STREAMS = 1
AHEAD = 5


def grid_kernel(
    recv, gain_hbm, thi_hbm, tlo_hbm, pick_hbm, out_hbm, *scratch
):
    acc = scratch[:STREAMS]
    gain, thi, tlo, pick, cells_v, cells_s, lost_v, wide_a, wide_b, yhi, ylo, zt, out, sems = scratch[
        STREAMS:
    ]
    groups, rows_in, _ = recv.shape
    capacity = rows_in - SUB
    lat_dev = gain.shape[0]
    blocks = gain.shape[2] // LANES
    half = lat_dev // 2
    loads = [
        pltpu.make_async_copy(src, dst, sems.at[1 + i])
        for i, (src, dst) in enumerate(
            (
                (gain_hbm.at[pl.ds(0, half)], gain.at[pl.ds(0, half)]),
                (gain_hbm.at[pl.ds(half, half)], gain.at[pl.ds(half, half)]),
                (thi_hbm, thi),
                (tlo_hbm, tlo),
                (pick_hbm, pick),
            )
        )
    ]
    for copy in loads:
        copy.start()

    bunches = groups // SUB
    bunches = groups // SUB
    cells = recv[:, capacity, :].astype(I32)
    cells_v[...] = cells
    cell_copy = pltpu.make_async_copy(cells_v, cells_s, sems.at[0])
    cell_copy.start()

    inner = lax.broadcasted_iota(I32, (SUB, LANES), 0)
    lane = lax.broadcasted_iota(I32, (SUB, LANES), 1)
    for bunch in range(bunches):
        x = cells[bunch * SUB : (bunch + 1) * SUB]
        lost = jnp.full(x.shape, -1, I32)
        place = (bunch * SUB + inner) * LANES + lane
        for d in range(1, SUB):
            later = (x == pltpu.roll(x, SUB - d, 0)) & (inner < SUB - d) & (lane >= capacity)
            lost = jnp.where(later, place, lost)
        lost_v[bunch * SUB : (bunch + 1) * SUB] = lost.astype(F32)

    def clear(i, carry):
        for a in acc:
            a[pl.ds(i * SUB, SUB)] = jnp.zeros((SUB, SUB, LANES), F32)
        return carry

    lax.fori_loop(0, acc[0].shape[0] // SUB, clear, 0)


    rows = groups * SUB
    weight = recv[:, capacity:, :].reshape(rows, LANES)
    lane = lax.broadcasted_iota(I32, (rows, LANES), 1)
    whi, wlo = split(weight)
    both = jnp.where(
        lane < capacity, whi.astype(F32), pltpu.roll(wlo.astype(F32), capacity, 1)
    ).astype(BF16)
    row = lax.broadcasted_iota(I32, (LANES, 2 * LANES), 0) % capacity
    col = lax.broadcasted_iota(I32, (LANES, 2 * LANES), 1) // LANES
    offset = row - col

    def widen(ref, k0):
        ones = jnp.where(offset == k0, 1.0, 0.0).astype(BF16)
        ref[...] = jnp.dot(both, ones, preferred_element_type=F32)

    def add_slots(ref, k0, bunch):
        for kk in range(2):
            into = acc[(kk * bunches + bunch) % STREAMS]
            sources = range(bunch * SUB, (bunch + 1) * SUB)
            cells = [cells_s[s, capacity + k0 + kk] for s in sources]
            old = [into[c] for c in cells]
            new = []
            for o, s in zip(old, sources):
                weights = ref[s * SUB : (s + 1) * SUB, kk * LANES : (kk + 1) * LANES]
                new.append(o + weights * recv[s, pl.ds(k0 + kk, 1), :])
            for c, value in zip(cells, new):
                into[c] = value

    widen(wide_a, 0)
    cell_copy.wait()

    def scatter(i, carry):
        k0 = 4 * i
        widen(wide_b, k0 + 2)
        for bunch in range(bunches):
            add_slots(wide_a, k0, bunch)
        widen(wide_a, k0 + 4)
        for bunch in range(bunches):
            add_slots(wide_b, k0 + 2, bunch)
        return carry

    lax.fori_loop(0, capacity // 4, scatter, 0)

    def last_below(bound):
        x = lost_v[...]
        return jnp.max(jnp.where(x < bound, x, -1.0))

    def repair(code):
        place = code.astype(I32)
        s, k = place // LANES, place % LANES - capacity
        weights = recv[s, capacity:, :]
        column = lax.broadcasted_iota(I32, weights.shape, 1) == k
        weights = jnp.sum(jnp.where(column, weights, 0.0), axis=1, keepdims=True)
        acc[0][cells_s[s, capacity + k]] += weights * recv[s, pl.ds(k, 1), :]
        return last_below(code)

    lax.while_loop(lambda code: code >= 0.0, repair, last_below(float(groups * LANES)))

    for copy in loads[:2]:
        copy.wait()

    width = blocks // RADIX * LANES
    pair = 2

    def transform(i, carry):
        r0 = i * pair
        for h in range(blocks // RADIX):
            xs = []
            for a in range(RADIX):
                b = a * (blocks // RADIX) + h
                parts = []
                for r in range(pair):
                    cell = (r0 + r) * blocks + b
                    total = acc[0][cell]
                    for t in range(1, STREAMS):
                        total = total + acc[t][cell]
                    parts.append(total * gain[r0 + r, :, b * LANES : (b + 1) * LANES])
                xs.append(jnp.concatenate(parts, axis=0))
            ys = real_fft(xs)
            rows = pl.ds(pl.multiple_of(r0 * SUB, pair * SUB), pair * SUB)
            for g in range(GROUPS):
                re, im = ys[g] if g else (ys[0][0], ys[RADIX // 2][0])
                for part, value in enumerate((re, im)):
                    lanes = pl.ds(part * width + h * LANES, LANES)
                    hi, lo = split(value)
                    yhi[g, rows, lanes] = hi
                    ylo[g, rows, lanes] = lo
        return carry

    lax.fori_loop(0, lat_dev // pair, transform, 0)
    for copy in loads[2:]:
        copy.wait()

    def dot(a, b):
        return jnp.dot(a, b, preferred_element_type=F32)

    waves = pick.shape[0]
    members = waves // GROUPS
    lane = lax.broadcasted_iota(I32, (2 * lat_dev * SUB, LANES), 1)
    open_tile = None
    for g in range(GROUPS):
        high, top = yhi[g], thi[g]
        z = dot(
            jnp.concatenate([high, high, ylo[g]], axis=1),
            jnp.concatenate([top, tlo[g], top], axis=0),
        )
        re = z[:, :LANES].reshape(lat_dev, 1, SUB, LANES)
        im = z[:, LANES:].reshape(lat_dev, 1, SUB, LANES)
        both = jnp.concatenate([re, im], axis=1).reshape(lat_dev * 2 * SUB, LANES)
        tile, offset = divmod(g * members, LANES)
        past = offset + members - LANES
        mine = jnp.where(lane >= offset, both, 0.0) if past > 0 else both
        open_tile = mine if open_tile is None else open_tile + mine
        if past >= 0:
            hi, lo = split(open_tile.T)
            zt[tile * LANES : (tile + 1) * LANES, :] = hi
            zt[waves + tile * LANES : waves + (tile + 1) * LANES, :] = lo
            open_tile = jnp.where(lane < past, both, 0.0) if past > 0 else None

    chunks = zt.shape[1] // LANES
    tall = LANES
    sends = []
    for j0 in range(0, waves, tall):
        sel = pick[j0 : j0 + tall, :]
        res = dot(jnp.concatenate([sel, sel], axis=1), zt[...])
        for jt in range(tall // SUB):
            for c in range(chunks):
                start = (j0 + jt * SUB) * chunks + c
                out[pl.ds(start, SUB, stride=chunks), :] = res[
                    jt * SUB : (jt + 1) * SUB, c * LANES : (c + 1) * LANES
                ]
        span = pl.ds(j0 * chunks, tall * chunks)
        sends.append(
            pltpu.make_async_copy(out.at[span], out_hbm.at[span], sems.at[6 + j0 // tall])
        )
        sends[-1].start()
    for copy in sends:
        copy.wait()


def grid_to_waves(recv, gain, thi, tlo, pick):
    lat_dev, ch_dev, lon_count = gain.shape
    waves = pick.shape[0]
    groups, capacity = recv.shape[0], recv.shape[1] - SUB
    cells = lat_dev * lon_count // LANES
    rows = lat_dev * ch_dev
    return pl.pallas_call(
        grid_kernel,
        out_shape=jax.ShapeDtypeStruct((waves * 2 * rows // LANES, LANES), F32),
        in_specs=[pl.BlockSpec(memory_space=pltpu.VMEM)]
        + [pl.BlockSpec(memory_space=pltpu.HBM)] * 4,
        out_specs=pl.BlockSpec(memory_space=pltpu.HBM),
        scratch_shapes=[pltpu.VMEM((cells, ch_dev, LANES), F32) for _ in range(STREAMS)]
        + [
            pltpu.VMEM(gain.shape, F32),
            pltpu.VMEM(thi.shape, BF16),
            pltpu.VMEM(tlo.shape, BF16),
            pltpu.VMEM(pick.shape, BF16),
            pltpu.VMEM((groups, LANES), I32),
            pltpu.SMEM((groups, LANES), I32),
            pltpu.VMEM((groups, LANES), F32),
            pltpu.VMEM((groups * SUB, 2 * LANES), F32),
            pltpu.VMEM((groups * SUB, 2 * LANES), F32),
            pltpu.VMEM((GROUPS, rows, thi.shape[1]), BF16),
            pltpu.VMEM((GROUPS, rows, thi.shape[1]), BF16),
            pltpu.VMEM((2 * waves, 2 * rows), BF16),
            pltpu.VMEM((waves * 2 * rows // LANES, LANES), F32),
            pltpu.SemaphoreType.DMA((6 + waves // LANES,)),
        ],
        compiler_params=pltpu.CompilerParams(vmem_limit_bytes=52 * MIB),
        name="grid_to_waves",
    )(recv, gain, thi, tlo, pick)


def prepare_kernel(lat_dev, band_ref, table_ref, hi_ref, lo_ref):
    grid_count = band_ref.shape[0]
    chunks = lat_dev // SUB
    full = LANES // grid_count
    assert chunks == full + 1
    half = 2 * SUB

    def body(c, carry):
        starts = [
            pl.multiple_of(band_ref[g] * lat_dev + c * SUB, SUB) for g in range(grid_count)
        ]
        for t in range(table_ref.shape[2] // LANES):
            lanes = pl.ds(t * LANES, LANES)
            for g0 in range(0, grid_count, half):
                turned = []
                for g1 in range(g0, g0 + half, SUB):
                    tiles = [
                        table_ref[0, pl.ds(starts[g], SUB), lanes] for g in range(g1, g1 + SUB)
                    ]
                    turned.append(jnp.swapaxes(jnp.stack(tiles), 0, 1))
                for k in range(SUB):
                    hi, lo = split(jnp.concatenate([x[k] for x in turned], axis=0))
                    start = jnp.where(
                        c < full, k * LANES + c * grid_count, full * SUB * grid_count + k * grid_count
                    )
                    start = pl.multiple_of(start + g0, half)
                    hi_ref[0, pl.ds(start, half), lanes] = hi
                    lo_ref[0, pl.ds(start, half), lanes] = lo
        return carry

    lax.fori_loop(0, chunks, body, 0)


def prepare_table(legendre, band_of, lat_dev):
    slot_count, lat_total, total_count = legendre.shape
    block = pl.BlockSpec((1, lat_total, total_count), lambda s: (s, 0, 0))
    return pl.pallas_call(
        functools.partial(prepare_kernel, lat_dev),
        grid=(slot_count,),
        out_shape=[jax.ShapeDtypeStruct(legendre.shape, BF16)] * 2,
        in_specs=[pl.BlockSpec(memory_space=pltpu.SMEM), block],
        out_specs=[block, block],
        compiler_params=pltpu.CompilerParams(vmem_limit_bytes=56 * MIB),
        cost_estimate=pl.CostEstimate(
            flops=4 * legendre.size, bytes_accessed=8 * legendre.size, transcendentals=0
        ),
        name="prepare_table",
    )(band_of, legendre)


def legendre_kernel(geo, x_ref, lhi_hbm, llo_hbm, out_hbm, lhi, llo, out, sems):
    grid_count, lev_count, slot_count, chunks = geo
    full = LANES // grid_count
    wide = 2 * SUB
    def loads(slot):
        return [
            pltpu.make_async_copy(src.at[slot], dst.at[slot], sems.at[2 * slot + i])
            for i, (src, dst) in enumerate(((lhi_hbm, lhi), (llo_hbm, llo)))
        ]

    for slot in range(AHEAD):
        for copy in loads(slot):
            copy.start()

    def store(slot):
        return pltpu.make_async_copy(
            out.at[slot], out_hbm.at[slot], sems.at[2 * slot_count + slot]
        )

    def body(slot, carry):
        lhs = []
        for lev in range(lev_count):
            pieces = []
            for c in range(chunks):
                start = (lev * slot_count + slot) * chunks + c
                pieces.append(
                    x_ref[pl.ds(start, grid_count, stride=lev_count * slot_count * chunks), :]
                )
            lhs.append(jnp.concatenate(pieces, axis=0).T)
        for copy in loads(slot):
            copy.wait()

        @pl.when(slot + AHEAD < slot_count)
        def _():
            for copy in loads(slot + AHEAD):
                copy.start()

        steps = range(LANES // wide)
        cut = full * grid_count
        main = [
            jnp.concatenate([m[k * wide : (k + 1) * wide, :cut] for m in lhs], axis=0) for k in steps
        ]
        rest = [
            jnp.concatenate([m[k * wide : (k + 1) * wide, cut:] for m in lhs], axis=0) for k in steps
        ]
        hi, lo = split(jnp.concatenate(main + rest, axis=1))
        both = jnp.concatenate([hi, lo], axis=0)
        prod = jnp.dot(both, lhi[slot], preferred_element_type=F32)
        tail = jnp.dot(hi, llo[slot], preferred_element_type=F32)
        total = prod[: hi.shape[0]] + (prod[hi.shape[0] :] + tail)
        for lev in range(lev_count):
            re = total[lev * wide : lev * wide + SUB]
            im = total[lev * wide + SUB : (lev + 1) * wide]
            out[slot, lev * SUB : (lev + 1) * SUB] = jnp.stack([re, im], axis=1)
        store(slot).start()
        return carry

    lax.fori_loop(0, slot_count, body, 0)
    for slot in range(slot_count):
        store(slot).wait()


def legendre_step(waves, lhi, llo, grid_count, lev_count):
    slot_count, lat_total, total_count = lhi.shape
    chunks = waves.shape[0] // (grid_count * lev_count * slot_count)
    geo = (grid_count, lev_count, slot_count, chunks)
    out_shape = (slot_count, lev_count * SUB, 2, total_count)
    return pl.pallas_call(
        functools.partial(legendre_kernel, geo),
        out_shape=jax.ShapeDtypeStruct(out_shape, F32),
        in_specs=[pl.BlockSpec(memory_space=pltpu.VMEM)]
        + [pl.BlockSpec(memory_space=pltpu.HBM)] * 2,
        out_specs=pl.BlockSpec(memory_space=pltpu.HBM),
        scratch_shapes=[
            pltpu.VMEM(lhi.shape, BF16),
            pltpu.VMEM(llo.shape, BF16),
            pltpu.VMEM(out_shape, F32),
            pltpu.SemaphoreType.DMA((3 * slot_count,)),
        ],
        compiler_params=pltpu.CompilerParams(vmem_limit_bytes=50 * MIB),
        name="legendre_step",
    )(waves, lhi, llo)


def shards(trajectory, legendre, obs_cell, obs_count, departure, obs_weight, band_of, m_order):
    grid_count = lax.axis_size("grid")
    lev_count = lax.axis_size("lev")
    ch_dev, lat_dev, lon_count = trajectory.shape
    slot_count, lat_total, total_count = legendre.shape
    wave_total = m_order.shape[0]
    cells_per_dev = lat_dev * lon_count // LANES

    sent = pack(obs_count, departure, obs_weight, obs_cell, cells_per_dev)
    recv = lax.all_to_all(sent, "grid", split_axis=0, concat_axis=0, tiled=True)

    gain = jnp.swapaxes(1.0 + 0.5 * jnp.tanh(trajectory), 0, 1)
    thi, tlo = split_np(wave_table(wave_total, lon_count))
    cols = wave_columns(wave_total).reshape(1, -1)
    pick = (m_order[:, None] == cols).astype(BF16)

    waves = grid_to_waves(recv, gain, jnp.asarray(thi), jnp.asarray(tlo), pick)
    outgoing = waves.reshape(grid_count * lev_count, 1, -1)
    incoming = lax.all_to_all(
        outgoing, ("grid", "lev"), split_axis=0, concat_axis=0, tiled=True
    )

    lhi, llo = prepare_table(legendre, band_of, lat_dev)
    return legendre_step(
        incoming.reshape(-1, LANES), lhi, llo, grid_count, lev_count
    )


def solution(mesh):
    placed = (
        P("lev", "grid", None),
        P(("grid", "lev"), None, None),
        P("grid"),
        P("grid"),
        P("grid", None),
        P("lev", "grid"),
        P(),
        P(),
    )
    return jax.shard_map(
        shards,
        mesh=mesh,
        in_specs=placed,
        out_specs=P(("grid", "lev"), None, None, None),
        check_vma=False,
    )
```

```python
import functools
import math

import jax
import jax.numpy as jnp
import numpy as np
from jax import lax
from jax.experimental import pallas as pl
from jax.experimental.pallas import tpu as pltpu
from jax.sharding import PartitionSpec as P

LANES = 128
SUB = 8
RADIX = 16
GROUPS = RADIX // 2
MIB = 1 << 20
F32 = jnp.float32
BF16 = jnp.bfloat16
I32 = jnp.int32


def wave_columns(wave_total):
    per_residue = wave_total // RADIX
    cols = np.zeros((GROUPS, 2 * per_residue), np.int32)
    for g in range(GROUPS):
        first, second = g, (RADIX - g if g else RADIX // 2)
        turns = RADIX * np.arange(per_residue)
        cols[g, :per_residue] = first + turns
        cols[g, per_residue : 2 * per_residue] = second + turns
    return cols


def wave_table(wave_total, lon_count):
    width = lon_count // RADIX
    cols = wave_columns(wave_total)
    per_residue = wave_total // RADIX
    fine = np.arange(width, dtype=np.int64)
    out = np.zeros((GROUPS, 2, width, 2, LANES), np.float64)
    for g in range(GROUPS):
        for i in range(2 * per_residue):
            m = int(cols[g, i])
            lane = (g * 2 * per_residue + i) % LANES
            angle = 2.0 * math.pi / lon_count * ((m * fine) % lon_count)
            factor = 1.0 if m == 0 else 2.0
            cos, sin = factor * np.cos(angle), factor * np.sin(angle)
            second = i >= per_residue
            if g == 0:
                part = 1 if second else 0
                out[g, part, :, 0, lane] = cos
                out[g, part, :, 1, lane] = -sin
            else:
                sign = -1.0 if second else 1.0
                out[g, 0, :, 0, lane] = cos
                out[g, 1, :, 0, lane] = sign * sin
                out[g, 0, :, 1, lane] = -sin
                out[g, 1, :, 1, lane] = sign * cos
    return out.reshape(GROUPS, 2 * width, 2 * LANES).astype(np.float32)


def split_np(table):
    high = table.astype(jnp.bfloat16)
    low = (table - high.astype(np.float32)).astype(jnp.bfloat16)
    return high, low


def split(x):
    high = x.astype(BF16)
    return high, (x - high.astype(F32)).astype(BF16)


def real_fft(xs):
    n = len(xs)
    if n == 2:
        return [(xs[0] + xs[1], None), (xs[0] - xs[1], None)]
    even, odd = real_fft(xs[0::2]), real_fft(xs[1::2])
    out = [None] * (n // 2 + 1)
    for k in range(n // 4 + 1):
        er, ei = even[k]
        orr, oi = odd[k]
        if k == 0:
            out[0] = (er + orr, None)
            out[n // 2] = (er - orr, None)
        elif 4 * k == n:
            out[k] = (er, -orr)
        else:
            c, s = math.cos(2 * math.pi * k / n), math.sin(2 * math.pi * k / n)
            if 8 * k == n:
                tr, ti = (orr + oi) * c, (oi - orr) * c
            else:
                tr, ti = orr * c + oi * s, oi * c - orr * s
            out[k] = (er + tr, ei + ti)
            out[n // 2 - k] = (er - tr, ti - ei)
    return out


def pack_kernel(
    capacity, cells_per_dev, count_hbm, dep_hbm, weight_hbm, cell_hbm, out_hbm,
    counts, weights, cells_v, out, sems,
):
    groups = out.shape[0]
    small = [
        pltpu.make_async_copy(src, dst, sems.at[i])
        for i, (src, dst) in enumerate(
            ((count_hbm, counts), (weight_hbm, weights), (cell_hbm, cells_v))
        )
    ]
    for copy in small:
        copy.start()
    parts = 4
    each = groups // parts
    large = [
        pltpu.make_async_copy(
            dep_hbm.at[pl.ds(i * each, each)],
            out.at[pl.ds(i * each, each), pl.ds(0, capacity)],
            sems.at[3 + i],
        )
        for i in range(parts)
    ]
    for copy in large:
        copy.start()
    for copy in small:
        copy.wait()
    lane = lax.broadcasted_iota(I32, (SUB, LANES), 1)
    for q in range(groups):
        tile = q // 2
        weight = weights[:, tile * LANES : (tile + 1) * LANES]
        cells = jnp.broadcast_to(cells_v[tile : tile + 1, :], (SUB, LANES))
        cells = (cells - q * cells_per_dev).astype(F32)
        if q % 2:
            weight = pltpu.roll(weight, capacity, 1)
        else:
            cells = pltpu.roll(cells, capacity, 1)
        live = jnp.where(lane < counts[q], 1.0, 0.0)
        out[q, capacity:, :] = jnp.where(lane < capacity, weight * live, cells)
    sends = []
    for i in range(parts):
        large[i].wait()
        span = pl.ds(i * each, each)
        sends.append(
            pltpu.make_async_copy(out.at[span], out_hbm.at[span], sems.at[3 + parts + i])
        )
        sends[-1].start()
    for copy in sends:
        copy.wait()


def pack(obs_count, departure, obs_weight, obs_cell, cells_per_dev):
    groups = obs_count.shape[0]
    slots = departure.shape[0]
    capacity = slots // groups
    assert 2 * capacity == LANES and obs_weight.shape[0] == SUB
    cell_rows = obs_cell.reshape(slots // LANES, LANES)
    out_shape = (groups, capacity + SUB, LANES)
    return pl.pallas_call(
        functools.partial(pack_kernel, capacity, cells_per_dev),
        out_shape=jax.ShapeDtypeStruct(out_shape, F32),
        in_specs=[pl.BlockSpec(memory_space=pltpu.HBM)] * 4,
        out_specs=pl.BlockSpec(memory_space=pltpu.HBM),
        scratch_shapes=[
            pltpu.SMEM(obs_count.shape, I32),
            pltpu.VMEM(obs_weight.shape, F32),
            pltpu.VMEM(cell_rows.shape, I32),
            pltpu.VMEM(out_shape, F32),
            pltpu.SemaphoreType.DMA((11,)),
        ],
        compiler_params=pltpu.CompilerParams(vmem_limit_bytes=60 * MIB),
        name="pack",
    )(obs_count, departure.reshape(groups, capacity, LANES), obs_weight, cell_rows)


STREAMS = 2
AHEAD = 5


def grid_kernel(
    recv, gain_hbm, thi_hbm, tlo_hbm, pick_hbm, out_hbm, *scratch
):
    acc = scratch[:STREAMS]
    gain, thi, tlo, pick, cells_v, cells_s, lost_v, wide_a, wide_b, yhi, ylo, zt, out, sems = scratch[
        STREAMS:
    ]
    groups, rows_in, _ = recv.shape
    capacity = rows_in - SUB
    lat_dev = gain.shape[0]
    blocks = gain.shape[2] // LANES
    half = lat_dev // 2
    loads = [
        pltpu.make_async_copy(src, dst, sems.at[1 + i])
        for i, (src, dst) in enumerate(
            (
                (gain_hbm.at[pl.ds(0, half)], gain.at[pl.ds(0, half)]),
                (gain_hbm.at[pl.ds(half, half)], gain.at[pl.ds(half, half)]),
                (thi_hbm, thi),
                (tlo_hbm, tlo),
                (pick_hbm, pick),
            )
        )
    ]
    for copy in loads:
        copy.start()

    bunches = groups // SUB
    bunches = groups // SUB
    cells = recv[:, capacity, :].astype(I32)
    cells_v[...] = cells
    cell_copy = pltpu.make_async_copy(cells_v, cells_s, sems.at[0])
    cell_copy.start()

    inner = lax.broadcasted_iota(I32, (SUB, LANES), 0)
    lane = lax.broadcasted_iota(I32, (SUB, LANES), 1)
    for bunch in range(bunches):
        x = cells[bunch * SUB : (bunch + 1) * SUB]
        lost = jnp.full(x.shape, -1, I32)
        place = (bunch * SUB + inner) * LANES + lane
        for d in range(STREAMS, SUB, STREAMS):
            later = (x == pltpu.roll(x, SUB - d, 0)) & (inner < SUB - d) & (lane >= capacity)
            lost = jnp.where(later, place, lost)
        lost_v[bunch * SUB : (bunch + 1) * SUB] = lost.astype(F32)

    def clear(i, carry):
        for a in acc:
            a[pl.ds(i * SUB, SUB)] = jnp.zeros((SUB, SUB, LANES), F32)
        return carry

    lax.fori_loop(0, acc[0].shape[0] // SUB, clear, 0)


    rows = groups * SUB
    weight = recv[:, capacity:, :].reshape(rows, LANES)
    lane = lax.broadcasted_iota(I32, (rows, LANES), 1)
    whi, wlo = split(weight)
    both = jnp.where(
        lane < capacity, whi.astype(F32), pltpu.roll(wlo.astype(F32), capacity, 1)
    ).astype(BF16)
    row = lax.broadcasted_iota(I32, (LANES, 2 * LANES), 0) % capacity
    col = lax.broadcasted_iota(I32, (LANES, 2 * LANES), 1) // LANES
    offset = row - col

    def widen(ref, k0):
        ones = jnp.where(offset == k0, 1.0, 0.0).astype(BF16)
        ref[...] = jnp.dot(both, ones, preferred_element_type=F32)

    def add_slots(ref, k0, bunch):
        for kk in range(2):
            sources = range(bunch * SUB, (bunch + 1) * SUB)
            cells = [cells_s[s, capacity + k0 + kk] for s in sources]
            old = [acc[i % STREAMS][c] for i, c in enumerate(cells)]
            new = []
            for o, s in zip(old, sources):
                weights = ref[s * SUB : (s + 1) * SUB, kk * LANES : (kk + 1) * LANES]
                new.append(o + weights * recv[s, pl.ds(k0 + kk, 1), :])
            for i, (c, value) in enumerate(zip(cells, new)):
                acc[i % STREAMS][c] = value

    widen(wide_a, 0)
    cell_copy.wait()

    def scatter(i, carry):
        k0 = 4 * i
        widen(wide_b, k0 + 2)
        for bunch in range(bunches):
            add_slots(wide_a, k0, bunch)
        widen(wide_a, k0 + 4)
        for bunch in range(bunches):
            add_slots(wide_b, k0 + 2, bunch)
        return carry

    lax.fori_loop(0, capacity // 4, scatter, 0)

    def last_below(bound):
        x = lost_v[...]
        return jnp.max(jnp.where(x < bound, x, -1.0))

    def repair(code):
        place = code.astype(I32)
        s, k = place // LANES, place % LANES - capacity
        weights = recv[s, capacity:, :]
        column = lax.broadcasted_iota(I32, weights.shape, 1) == k
        weights = jnp.sum(jnp.where(column, weights, 0.0), axis=1, keepdims=True)
        acc[0][cells_s[s, capacity + k]] += weights * recv[s, pl.ds(k, 1), :]
        return last_below(code)

    lax.while_loop(lambda code: code >= 0.0, repair, last_below(float(groups * LANES)))

    for copy in loads[:2]:
        copy.wait()

    width = blocks // RADIX * LANES
    pair = 2

    def transform(i, carry):
        r0 = i * pair
        for h in range(blocks // RADIX):
            xs = []
            for a in range(RADIX):
                b = a * (blocks // RADIX) + h
                parts = []
                for r in range(pair):
                    cell = (r0 + r) * blocks + b
                    total = acc[0][cell]
                    for t in range(1, STREAMS):
                        total = total + acc[t][cell]
                    parts.append(total * gain[r0 + r, :, b * LANES : (b + 1) * LANES])
                xs.append(jnp.concatenate(parts, axis=0))
            ys = real_fft(xs)
            rows = pl.ds(pl.multiple_of(r0 * SUB, pair * SUB), pair * SUB)
            for g in range(GROUPS):
                re, im = ys[g] if g else (ys[0][0], ys[RADIX // 2][0])
                for part, value in enumerate((re, im)):
                    lanes = pl.ds(part * width + h * LANES, LANES)
                    hi, lo = split(value)
                    yhi[g, rows, lanes] = hi
                    ylo[g, rows, lanes] = lo
        return carry

    lax.fori_loop(0, lat_dev // pair, transform, 0)
    for copy in loads[2:]:
        copy.wait()

    def dot(a, b):
        return jnp.dot(a, b, preferred_element_type=F32)

    waves = pick.shape[0]
    members = waves // GROUPS
    lane = lax.broadcasted_iota(I32, (2 * lat_dev * SUB, LANES), 1)
    open_tile = None
    for g in range(GROUPS):
        high, top = yhi[g], thi[g]
        z = dot(
            jnp.concatenate([high, high, ylo[g]], axis=1),
            jnp.concatenate([top, tlo[g], top], axis=0),
        )
        re = z[:, :LANES].reshape(lat_dev, 1, SUB, LANES)
        im = z[:, LANES:].reshape(lat_dev, 1, SUB, LANES)
        both = jnp.concatenate([re, im], axis=1).reshape(lat_dev * 2 * SUB, LANES)
        tile, offset = divmod(g * members, LANES)
        past = offset + members - LANES
        mine = jnp.where(lane >= offset, both, 0.0) if past > 0 else both
        open_tile = mine if open_tile is None else open_tile + mine
        if past >= 0:
            hi, lo = split(open_tile.T)
            zt[tile * LANES : (tile + 1) * LANES, :] = hi
            zt[waves + tile * LANES : waves + (tile + 1) * LANES, :] = lo
            open_tile = jnp.where(lane < past, both, 0.0) if past > 0 else None

    chunks = zt.shape[1] // LANES
    tall = LANES
    sends = []
    for j0 in range(0, waves, tall):
        sel = pick[j0 : j0 + tall, :]
        res = dot(jnp.concatenate([sel, sel], axis=1), zt[...])
        for jt in range(tall // SUB):
            for c in range(chunks):
                start = (j0 + jt * SUB) * chunks + c
                out[pl.ds(start, SUB, stride=chunks), :] = res[
                    jt * SUB : (jt + 1) * SUB, c * LANES : (c + 1) * LANES
                ]
        span = pl.ds(j0 * chunks, tall * chunks)
        sends.append(
            pltpu.make_async_copy(out.at[span], out_hbm.at[span], sems.at[6 + j0 // tall])
        )
        sends[-1].start()
    for copy in sends:
        copy.wait()


def grid_to_waves(recv, gain, thi, tlo, pick):
    lat_dev, ch_dev, lon_count = gain.shape
    waves = pick.shape[0]
    groups, capacity = recv.shape[0], recv.shape[1] - SUB
    cells = lat_dev * lon_count // LANES
    rows = lat_dev * ch_dev
    return pl.pallas_call(
        grid_kernel,
        out_shape=jax.ShapeDtypeStruct((waves * 2 * rows // LANES, LANES), F32),
        in_specs=[pl.BlockSpec(memory_space=pltpu.VMEM)]
        + [pl.BlockSpec(memory_space=pltpu.HBM)] * 4,
        out_specs=pl.BlockSpec(memory_space=pltpu.HBM),
        scratch_shapes=[pltpu.VMEM((cells, ch_dev, LANES), F32) for _ in range(STREAMS)]
        + [
            pltpu.VMEM(gain.shape, F32),
            pltpu.VMEM(thi.shape, BF16),
            pltpu.VMEM(tlo.shape, BF16),
            pltpu.VMEM(pick.shape, BF16),
            pltpu.VMEM((groups, LANES), I32),
            pltpu.SMEM((groups, LANES), I32),
            pltpu.VMEM((groups, LANES), F32),
            pltpu.VMEM((groups * SUB, 2 * LANES), F32),
            pltpu.VMEM((groups * SUB, 2 * LANES), F32),
            pltpu.VMEM((GROUPS, rows, thi.shape[1]), BF16),
            pltpu.VMEM((GROUPS, rows, thi.shape[1]), BF16),
            pltpu.VMEM((2 * waves, 2 * rows), BF16),
            pltpu.VMEM((waves * 2 * rows // LANES, LANES), F32),
            pltpu.SemaphoreType.DMA((6 + waves // LANES,)),
        ],
        compiler_params=pltpu.CompilerParams(vmem_limit_bytes=52 * MIB),
        name="grid_to_waves",
    )(recv, gain, thi, tlo, pick)


def prepare_kernel(lat_dev, band_ref, table_ref, hi_ref, lo_ref):
    grid_count = band_ref.shape[0]
    chunks = lat_dev // SUB
    full = LANES // grid_count
    assert chunks == full + 1
    half = 2 * SUB

    def body(c, carry):
        starts = [
            pl.multiple_of(band_ref[g] * lat_dev + c * SUB, SUB) for g in range(grid_count)
        ]
        for t in range(table_ref.shape[2] // LANES):
            lanes = pl.ds(t * LANES, LANES)
            for g0 in range(0, grid_count, half):
                turned = []
                for g1 in range(g0, g0 + half, SUB):
                    tiles = [
                        table_ref[0, pl.ds(starts[g], SUB), lanes] for g in range(g1, g1 + SUB)
                    ]
                    turned.append(jnp.swapaxes(jnp.stack(tiles), 0, 1))
                for k in range(SUB):
                    hi, lo = split(jnp.concatenate([x[k] for x in turned], axis=0))
                    start = jnp.where(
                        c < full, k * LANES + c * grid_count, full * SUB * grid_count + k * grid_count
                    )
                    start = pl.multiple_of(start + g0, half)
                    hi_ref[0, pl.ds(start, half), lanes] = hi
                    lo_ref[0, pl.ds(start, half), lanes] = lo
        return carry

    lax.fori_loop(0, chunks, body, 0)


def prepare_table(legendre, band_of, lat_dev):
    slot_count, lat_total, total_count = legendre.shape
    block = pl.BlockSpec((1, lat_total, total_count), lambda s: (s, 0, 0))
    return pl.pallas_call(
        functools.partial(prepare_kernel, lat_dev),
        grid=(slot_count,),
        out_shape=[jax.ShapeDtypeStruct(legendre.shape, BF16)] * 2,
        in_specs=[pl.BlockSpec(memory_space=pltpu.SMEM), block],
        out_specs=[block, block],
        compiler_params=pltpu.CompilerParams(vmem_limit_bytes=56 * MIB),
        cost_estimate=pl.CostEstimate(
            flops=4 * legendre.size, bytes_accessed=8 * legendre.size, transcendentals=0
        ),
        name="prepare_table",
    )(band_of, legendre)


def legendre_kernel(geo, x_ref, lhi_hbm, llo_hbm, out_hbm, lhi, llo, out, sems):
    grid_count, lev_count, slot_count, chunks = geo
    full = LANES // grid_count
    wide = 2 * SUB
    def loads(slot):
        return [
            pltpu.make_async_copy(src.at[slot], dst.at[slot], sems.at[2 * slot + i])
            for i, (src, dst) in enumerate(((lhi_hbm, lhi), (llo_hbm, llo)))
        ]

    for slot in range(AHEAD):
        for copy in loads(slot):
            copy.start()

    def store(slot):
        return pltpu.make_async_copy(
            out.at[slot], out_hbm.at[slot], sems.at[2 * slot_count + slot]
        )

    def body(slot, carry):
        lhs = []
        for lev in range(lev_count):
            pieces = []
            for c in range(chunks):
                start = (lev * slot_count + slot) * chunks + c
                pieces.append(
                    x_ref[pl.ds(start, grid_count, stride=lev_count * slot_count * chunks), :]
                )
            lhs.append(jnp.concatenate(pieces, axis=0).T)
        for copy in loads(slot):
            copy.wait()

        @pl.when(slot + AHEAD < slot_count)
        def _():
            for copy in loads(slot + AHEAD):
                copy.start()

        steps = range(LANES // wide)
        cut = full * grid_count
        main = [
            jnp.concatenate([m[k * wide : (k + 1) * wide, :cut] for m in lhs], axis=0) for k in steps
        ]
        rest = [
            jnp.concatenate([m[k * wide : (k + 1) * wide, cut:] for m in lhs], axis=0) for k in steps
        ]
        hi, lo = split(jnp.concatenate(main + rest, axis=1))
        both = jnp.concatenate([hi, lo], axis=0)
        prod = jnp.dot(both, lhi[slot], preferred_element_type=F32)
        tail = jnp.dot(hi, llo[slot], preferred_element_type=F32)
        total = prod[: hi.shape[0]] + (prod[hi.shape[0] :] + tail)
        for lev in range(lev_count):
            re = total[lev * wide : lev * wide + SUB]
            im = total[lev * wide + SUB : (lev + 1) * wide]
            out[slot, lev * SUB : (lev + 1) * SUB] = jnp.stack([re, im], axis=1)
        store(slot).start()
        return carry

    lax.fori_loop(0, slot_count, body, 0)
    for slot in range(slot_count):
        store(slot).wait()


def legendre_step(waves, lhi, llo, grid_count, lev_count):
    slot_count, lat_total, total_count = lhi.shape
    chunks = waves.shape[0] // (grid_count * lev_count * slot_count)
    geo = (grid_count, lev_count, slot_count, chunks)
    out_shape = (slot_count, lev_count * SUB, 2, total_count)
    return pl.pallas_call(
        functools.partial(legendre_kernel, geo),
        out_shape=jax.ShapeDtypeStruct(out_shape, F32),
        in_specs=[pl.BlockSpec(memory_space=pltpu.VMEM)]
        + [pl.BlockSpec(memory_space=pltpu.HBM)] * 2,
        out_specs=pl.BlockSpec(memory_space=pltpu.HBM),
        scratch_shapes=[
            pltpu.VMEM(lhi.shape, BF16),
            pltpu.VMEM(llo.shape, BF16),
            pltpu.VMEM(out_shape, F32),
            pltpu.SemaphoreType.DMA((3 * slot_count,)),
        ],
        compiler_params=pltpu.CompilerParams(vmem_limit_bytes=50 * MIB),
        name="legendre_step",
    )(waves, lhi, llo)


def shards(trajectory, legendre, obs_cell, obs_count, departure, obs_weight, band_of, m_order):
    grid_count = lax.axis_size("grid")
    lev_count = lax.axis_size("lev")
    ch_dev, lat_dev, lon_count = trajectory.shape
    slot_count, lat_total, total_count = legendre.shape
    wave_total = m_order.shape[0]
    cells_per_dev = lat_dev * lon_count // LANES

    sent = pack(obs_count, departure, obs_weight, obs_cell, cells_per_dev)
    recv = lax.all_to_all(sent, "grid", split_axis=0, concat_axis=0, tiled=True)

    gain = jnp.swapaxes(1.0 + 0.5 * jnp.tanh(trajectory), 0, 1)
    thi, tlo = split_np(wave_table(wave_total, lon_count))
    cols = wave_columns(wave_total).reshape(1, -1)
    pick = (m_order[:, None] == cols).astype(BF16)

    waves = grid_to_waves(recv, gain, jnp.asarray(thi), jnp.asarray(tlo), pick)
    outgoing = waves.reshape(grid_count * lev_count, 1, -1)
    incoming = lax.all_to_all(
        outgoing, ("grid", "lev"), split_axis=0, concat_axis=0, tiled=True
    )

    lhi, llo = prepare_table(legendre, band_of, lat_dev)
    return legendre_step(
        incoming.reshape(-1, LANES), lhi, llo, grid_count, lev_count
    )


def solution(mesh):
    placed = (
        P("lev", "grid", None),
        P(("grid", "lev"), None, None),
        P("grid"),
        P("grid"),
        P("grid", None),
        P("lev", "grid"),
        P(),
        P(),
    )
    return jax.shard_map(
        shards,
        mesh=mesh,
        in_specs=placed,
        out_specs=P(("grid", "lev"), None, None, None),
        check_vma=False,
    )
```

```python
import functools
import math

import jax
import jax.numpy as jnp
import numpy as np
from jax import lax
from jax.experimental import pallas as pl
from jax.experimental.pallas import tpu as pltpu
from jax.sharding import PartitionSpec as P

LANES = 128
SUB = 8
RADIX = 16
GROUPS = RADIX // 2
MIB = 1 << 20
F32 = jnp.float32
BF16 = jnp.bfloat16
I32 = jnp.int32


def wave_columns(wave_total):
    per_residue = wave_total // RADIX
    cols = np.zeros((GROUPS, 2 * per_residue), np.int32)
    for g in range(GROUPS):
        first, second = g, (RADIX - g if g else RADIX // 2)
        turns = RADIX * np.arange(per_residue)
        cols[g, :per_residue] = first + turns
        cols[g, per_residue : 2 * per_residue] = second + turns
    return cols


def wave_table(wave_total, lon_count):
    width = lon_count // RADIX
    cols = wave_columns(wave_total)
    per_residue = wave_total // RADIX
    fine = np.arange(width, dtype=np.int64)
    out = np.zeros((GROUPS, 2, width, 2, LANES), np.float64)
    for g in range(GROUPS):
        for i in range(2 * per_residue):
            m = int(cols[g, i])
            lane = (g * 2 * per_residue + i) % LANES
            angle = 2.0 * math.pi / lon_count * ((m * fine) % lon_count)
            factor = 1.0 if m == 0 else 2.0
            cos, sin = factor * np.cos(angle), factor * np.sin(angle)
            second = i >= per_residue
            if g == 0:
                part = 1 if second else 0
                out[g, part, :, 0, lane] = cos
                out[g, part, :, 1, lane] = -sin
            else:
                sign = -1.0 if second else 1.0
                out[g, 0, :, 0, lane] = cos
                out[g, 1, :, 0, lane] = sign * sin
                out[g, 0, :, 1, lane] = -sin
                out[g, 1, :, 1, lane] = sign * cos
    return out.reshape(GROUPS, 2 * width, 2 * LANES).astype(np.float32)


def split_np(table):
    high = table.astype(jnp.bfloat16)
    low = (table - high.astype(np.float32)).astype(jnp.bfloat16)
    return high, low


def split(x):
    high = x.astype(BF16)
    return high, (x - high.astype(F32)).astype(BF16)


def real_fft(xs):
    n = len(xs)
    if n == 2:
        return [(xs[0] + xs[1], None), (xs[0] - xs[1], None)]
    even, odd = real_fft(xs[0::2]), real_fft(xs[1::2])
    out = [None] * (n // 2 + 1)
    for k in range(n // 4 + 1):
        er, ei = even[k]
        orr, oi = odd[k]
        if k == 0:
            out[0] = (er + orr, None)
            out[n // 2] = (er - orr, None)
        elif 4 * k == n:
            out[k] = (er, -orr)
        else:
            c, s = math.cos(2 * math.pi * k / n), math.sin(2 * math.pi * k / n)
            if 8 * k == n:
                tr, ti = (orr + oi) * c, (oi - orr) * c
            else:
                tr, ti = orr * c + oi * s, oi * c - orr * s
            out[k] = (er + tr, ei + ti)
            out[n // 2 - k] = (er - tr, ti - ei)
    return out


def pack_kernel(
    capacity, cells_per_dev, count_hbm, dep_hbm, weight_hbm, cell_hbm, out_hbm,
    counts, weights, cells_v, out, sems,
):
    groups = out.shape[0]
    small = [
        pltpu.make_async_copy(src, dst, sems.at[i])
        for i, (src, dst) in enumerate(
            ((count_hbm, counts), (weight_hbm, weights), (cell_hbm, cells_v))
        )
    ]
    for copy in small:
        copy.start()
    parts = 4
    each = groups // parts
    large = [
        pltpu.make_async_copy(
            dep_hbm.at[pl.ds(i * each, each)],
            out.at[pl.ds(i * each, each), pl.ds(0, capacity)],
            sems.at[3 + i],
        )
        for i in range(parts)
    ]
    for copy in large:
        copy.start()
    for copy in small:
        copy.wait()
    lane = lax.broadcasted_iota(I32, (SUB, LANES), 1)
    for q in range(groups):
        tile = q // 2
        weight = weights[:, tile * LANES : (tile + 1) * LANES]
        cells = jnp.broadcast_to(cells_v[tile : tile + 1, :], (SUB, LANES))
        cells = (cells - q * cells_per_dev).astype(F32)
        if q % 2:
            weight = pltpu.roll(weight, capacity, 1)
        else:
            cells = pltpu.roll(cells, capacity, 1)
        live = jnp.where(lane < counts[q], 1.0, 0.0)
        out[q, capacity:, :] = jnp.where(lane < capacity, weight * live, cells)
    sends = []
    for i in range(parts):
        large[i].wait()
        span = pl.ds(i * each, each)
        sends.append(
            pltpu.make_async_copy(out.at[span], out_hbm.at[span], sems.at[3 + parts + i])
        )
        sends[-1].start()
    for copy in sends:
        copy.wait()


def pack(obs_count, departure, obs_weight, obs_cell, cells_per_dev):
    groups = obs_count.shape[0]
    slots = departure.shape[0]
    capacity = slots // groups
    assert 2 * capacity == LANES and obs_weight.shape[0] == SUB
    cell_rows = obs_cell.reshape(slots // LANES, LANES)
    out_shape = (groups, capacity + SUB, LANES)
    return pl.pallas_call(
        functools.partial(pack_kernel, capacity, cells_per_dev),
        out_shape=jax.ShapeDtypeStruct(out_shape, F32),
        in_specs=[pl.BlockSpec(memory_space=pltpu.HBM)] * 4,
        out_specs=pl.BlockSpec(memory_space=pltpu.HBM),
        scratch_shapes=[
            pltpu.SMEM(obs_count.shape, I32),
            pltpu.VMEM(obs_weight.shape, F32),
            pltpu.VMEM(cell_rows.shape, I32),
            pltpu.VMEM(out_shape, F32),
            pltpu.SemaphoreType.DMA((11,)),
        ],
        compiler_params=pltpu.CompilerParams(vmem_limit_bytes=60 * MIB),
        name="pack",
    )(obs_count, departure.reshape(groups, capacity, LANES), obs_weight, cell_rows)


STREAMS = 1
AHEAD = 5
PIECES = 4


def grid_kernel(
    recv, gain_hbm, thi_hbm, tlo_hbm, pick_hbm, out_hbm, *scratch
):
    acc = scratch[:STREAMS]
    gain, thi, tlo, pick, cells_v, cells_s, lost_v, wide_a, wide_b, yhi, ylo, zt, out, sems = scratch[
        STREAMS:
    ]
    groups, rows_in, _ = recv.shape
    capacity = rows_in - SUB
    lat_dev = gain.shape[0]
    blocks = gain.shape[2] // LANES
    half = lat_dev // 2
    loads = [
        pltpu.make_async_copy(src, dst, sems.at[1 + i])
        for i, (src, dst) in enumerate(
            (
                (gain_hbm.at[pl.ds(0, half)], gain.at[pl.ds(0, half)]),
                (gain_hbm.at[pl.ds(half, half)], gain.at[pl.ds(half, half)]),
                (thi_hbm, thi),
                (tlo_hbm, tlo),
                (pick_hbm, pick),
            )
        )
    ]
    for copy in loads:
        copy.start()

    bunches = groups // SUB
    bunches = groups // SUB
    cells = recv[:, capacity, :].astype(I32)
    cells_v[...] = cells
    cell_copy = pltpu.make_async_copy(cells_v, cells_s, sems.at[0])
    cell_copy.start()

    inner = lax.broadcasted_iota(I32, (SUB, LANES), 0)
    lane = lax.broadcasted_iota(I32, (SUB, LANES), 1)
    for bunch in range(bunches):
        x = cells[bunch * SUB : (bunch + 1) * SUB]
        lost = jnp.full(x.shape, -1, I32)
        place = (bunch * SUB + inner) * LANES + lane
        for d in range(1, SUB):
            later = (x == pltpu.roll(x, SUB - d, 0)) & (inner < SUB - d) & (lane >= capacity)
            lost = jnp.where(later, place, lost)
        lost_v[bunch * SUB : (bunch + 1) * SUB] = lost.astype(F32)

    def clear(i, carry):
        for a in acc:
            a[pl.ds(i * SUB, SUB)] = jnp.zeros((SUB, SUB, LANES), F32)
        return carry

    lax.fori_loop(0, acc[0].shape[0] // SUB, clear, 0)


    rows = groups * SUB
    weight = recv[:, capacity:, :].reshape(rows, LANES)
    lane = lax.broadcasted_iota(I32, (rows, LANES), 1)
    whi, wlo = split(weight)
    both = jnp.where(
        lane < capacity, whi.astype(F32), pltpu.roll(wlo.astype(F32), capacity, 1)
    ).astype(BF16)
    row = lax.broadcasted_iota(I32, (LANES, 2 * LANES), 0) % capacity
    col = lax.broadcasted_iota(I32, (LANES, 2 * LANES), 1) // LANES
    offset = row - col

    def widen(ref, k0):
        ones = jnp.where(offset == k0, 1.0, 0.0).astype(BF16)
        ref[...] = jnp.dot(both, ones, preferred_element_type=F32)

    def add_slots(ref, k0, bunch):
        for kk in range(2):
            into = acc[(kk * bunches + bunch) % STREAMS]
            sources = range(bunch * SUB, (bunch + 1) * SUB)
            cells = [cells_s[s, capacity + k0 + kk] for s in sources]
            old = [into[c] for c in cells]
            new = []
            for o, s in zip(old, sources):
                weights = ref[s * SUB : (s + 1) * SUB, kk * LANES : (kk + 1) * LANES]
                new.append(o + weights * recv[s, pl.ds(k0 + kk, 1), :])
            for c, value in zip(cells, new):
                into[c] = value

    widen(wide_a, 0)
    cell_copy.wait()

    def scatter(i, carry):
        k0 = 4 * i
        widen(wide_b, k0 + 2)
        for bunch in range(bunches):
            add_slots(wide_a, k0, bunch)
        widen(wide_a, k0 + 4)
        for bunch in range(bunches):
            add_slots(wide_b, k0 + 2, bunch)
        return carry

    lax.fori_loop(0, capacity // 4, scatter, 0)

    def last_below(bound):
        x = lost_v[...]
        return jnp.max(jnp.where(x < bound, x, -1.0))

    def repair(code):
        place = code.astype(I32)
        s, k = place // LANES, place % LANES - capacity
        weights = recv[s, capacity:, :]
        column = lax.broadcasted_iota(I32, weights.shape, 1) == k
        weights = jnp.sum(jnp.where(column, weights, 0.0), axis=1, keepdims=True)
        acc[0][cells_s[s, capacity + k]] += weights * recv[s, pl.ds(k, 1), :]
        return last_below(code)

    lax.while_loop(lambda code: code >= 0.0, repair, last_below(float(groups * LANES)))

    for copy in loads[:2]:
        copy.wait()

    width = blocks // RADIX * LANES
    pair = 2

    def transform(i, carry):
        r0 = i * pair
        for h in range(blocks // RADIX):
            xs = []
            for a in range(RADIX):
                b = a * (blocks // RADIX) + h
                parts = []
                for r in range(pair):
                    cell = (r0 + r) * blocks + b
                    total = acc[0][cell]
                    for t in range(1, STREAMS):
                        total = total + acc[t][cell]
                    parts.append(total * gain[r0 + r, :, b * LANES : (b + 1) * LANES])
                xs.append(jnp.concatenate(parts, axis=0))
            ys = real_fft(xs)
            rows = pl.ds(pl.multiple_of(r0 * SUB, pair * SUB), pair * SUB)
            for g in range(GROUPS):
                re, im = ys[g] if g else (ys[0][0], ys[RADIX // 2][0])
                for part, value in enumerate((re, im)):
                    lanes = pl.ds(part * width + h * LANES, LANES)
                    hi, lo = split(value)
                    yhi[g, rows, lanes] = hi
                    ylo[g, rows, lanes] = lo
        return carry

    lax.fori_loop(0, lat_dev // pair, transform, 0)
    for copy in loads[2:]:
        copy.wait()

    def dot(a, b):
        return jnp.dot(a, b, preferred_element_type=F32)

    waves = pick.shape[0]
    members = waves // GROUPS
    lane = lax.broadcasted_iota(I32, (2 * lat_dev * SUB, LANES), 1)
    open_tile = None
    for g in range(GROUPS):
        high, top = yhi[g], thi[g]
        z = dot(
            jnp.concatenate([high, high, ylo[g]], axis=1),
            jnp.concatenate([top, tlo[g], top], axis=0),
        )
        re = z[:, :LANES].reshape(lat_dev, 1, SUB, LANES)
        im = z[:, LANES:].reshape(lat_dev, 1, SUB, LANES)
        both = jnp.concatenate([re, im], axis=1).reshape(lat_dev * 2 * SUB, LANES)
        tile, offset = divmod(g * members, LANES)
        past = offset + members - LANES
        mine = jnp.where(lane >= offset, both, 0.0) if past > 0 else both
        open_tile = mine if open_tile is None else open_tile + mine
        if past >= 0:
            hi, lo = split(open_tile.T)
            zt[tile * LANES : (tile + 1) * LANES, :] = hi
            zt[waves + tile * LANES : waves + (tile + 1) * LANES, :] = lo
            open_tile = jnp.where(lane < past, both, 0.0) if past > 0 else None

    chunks = zt.shape[1] // LANES
    tall = LANES
    sends = []
    for j0 in range(0, waves, tall):
        sel = pick[j0 : j0 + tall, :]
        res = dot(jnp.concatenate([sel, sel], axis=1), zt[...])
        for jt in range(tall // SUB):
            for c in range(chunks):
                start = (j0 + jt * SUB) * chunks + c
                out[pl.ds(start, SUB, stride=chunks), :] = res[
                    jt * SUB : (jt + 1) * SUB, c * LANES : (c + 1) * LANES
                ]
        span = pl.ds(j0 * chunks, tall * chunks)
        sends.append(
            pltpu.make_async_copy(out.at[span], out_hbm.at[span], sems.at[6 + j0 // tall])
        )
        sends[-1].start()
    for copy in sends:
        copy.wait()


def grid_to_waves(recv, gain, thi, tlo, pick):
    lat_dev, ch_dev, lon_count = gain.shape
    waves = pick.shape[0]
    groups, capacity = recv.shape[0], recv.shape[1] - SUB
    cells = lat_dev * lon_count // LANES
    rows = lat_dev * ch_dev
    return pl.pallas_call(
        grid_kernel,
        out_shape=jax.ShapeDtypeStruct((waves * 2 * rows // LANES, LANES), F32),
        in_specs=[pl.BlockSpec(memory_space=pltpu.VMEM)]
        + [pl.BlockSpec(memory_space=pltpu.HBM)] * 4,
        out_specs=pl.BlockSpec(memory_space=pltpu.HBM),
        scratch_shapes=[pltpu.VMEM((cells, ch_dev, LANES), F32) for _ in range(STREAMS)]
        + [
            pltpu.VMEM(gain.shape, F32),
            pltpu.VMEM(thi.shape, BF16),
            pltpu.VMEM(tlo.shape, BF16),
            pltpu.VMEM(pick.shape, BF16),
            pltpu.VMEM((groups, LANES), I32),
            pltpu.SMEM((groups, LANES), I32),
            pltpu.VMEM((groups, LANES), F32),
            pltpu.VMEM((groups * SUB, 2 * LANES), F32),
            pltpu.VMEM((groups * SUB, 2 * LANES), F32),
            pltpu.VMEM((GROUPS, rows, thi.shape[1]), BF16),
            pltpu.VMEM((GROUPS, rows, thi.shape[1]), BF16),
            pltpu.VMEM((2 * waves, 2 * rows), BF16),
            pltpu.VMEM((waves * 2 * rows // LANES, LANES), F32),
            pltpu.SemaphoreType.DMA((6 + waves // LANES,)),
        ],
        compiler_params=pltpu.CompilerParams(vmem_limit_bytes=52 * MIB),
        name="grid_to_waves",
    )(recv, gain, thi, tlo, pick)


def prepare_kernel(lat_dev, band_ref, table_ref, hi_ref, lo_ref):
    grid_count = band_ref.shape[0]
    chunks = lat_dev // SUB
    full = LANES // grid_count
    assert chunks == full + 1
    half = 2 * SUB

    def body(c, carry):
        starts = [
            pl.multiple_of(band_ref[g] * lat_dev + c * SUB, SUB) for g in range(grid_count)
        ]
        for t in range(table_ref.shape[2] // LANES):
            lanes = pl.ds(t * LANES, LANES)
            for g0 in range(0, grid_count, half):
                turned = []
                for g1 in range(g0, g0 + half, SUB):
                    tiles = [
                        table_ref[0, pl.ds(starts[g], SUB), lanes] for g in range(g1, g1 + SUB)
                    ]
                    turned.append(jnp.swapaxes(jnp.stack(tiles), 0, 1))
                for k in range(SUB):
                    hi, lo = split(jnp.concatenate([x[k] for x in turned], axis=0))
                    start = jnp.where(
                        c < full, k * LANES + c * grid_count, full * SUB * grid_count + k * grid_count
                    )
                    start = pl.multiple_of(start + g0, half)
                    hi_ref[0, pl.ds(start, half), lanes] = hi
                    lo_ref[0, pl.ds(start, half), lanes] = lo
        return carry

    lax.fori_loop(0, chunks, body, 0)


def prepare_table(legendre, band_of, lat_dev):
    slot_count, lat_total, total_count = legendre.shape
    block = pl.BlockSpec((1, lat_total, total_count), lambda s: (s, 0, 0))
    return pl.pallas_call(
        functools.partial(prepare_kernel, lat_dev),
        grid=(slot_count,),
        out_shape=[jax.ShapeDtypeStruct(legendre.shape, BF16)] * 2,
        in_specs=[pl.BlockSpec(memory_space=pltpu.SMEM), block],
        out_specs=[block, block],
        compiler_params=pltpu.CompilerParams(vmem_limit_bytes=56 * MIB),
        cost_estimate=pl.CostEstimate(
            flops=4 * legendre.size, bytes_accessed=8 * legendre.size, transcendentals=0
        ),
        name="prepare_table",
    )(band_of, legendre)


def legendre_kernel(geo, x_ref, lhi_hbm, llo_hbm, out_hbm, lhi, llo, out, sems):
    grid_count, lev_count, slot_count, chunks = geo
    full = LANES // grid_count
    wide = 2 * SUB
    def loads(slot):
        part = lhi.shape[1] // PIECES
        return [
            pltpu.make_async_copy(
                src.at[slot, pl.ds(j * part, part)],
                dst.at[slot, pl.ds(j * part, part)],
                sems.at[(2 * slot + i) * PIECES + j],
            )
            for i, (src, dst) in enumerate(((lhi_hbm, lhi), (llo_hbm, llo)))
            for j in range(PIECES)
        ]

    for slot in range(AHEAD):
        for copy in loads(slot):
            copy.start()

    def store(slot):
        return pltpu.make_async_copy(
            out.at[slot], out_hbm.at[slot], sems.at[2 * PIECES * slot_count + slot]
        )

    def body(slot, carry):
        lhs = []
        for lev in range(lev_count):
            pieces = []
            for c in range(chunks):
                start = (lev * slot_count + slot) * chunks + c
                pieces.append(
                    x_ref[pl.ds(start, grid_count, stride=lev_count * slot_count * chunks), :]
                )
            lhs.append(jnp.concatenate(pieces, axis=0).T)
        for copy in loads(slot):
            copy.wait()

        @pl.when(slot + AHEAD < slot_count)
        def _():
            for copy in loads(slot + AHEAD):
                copy.start()

        steps = range(LANES // wide)
        cut = full * grid_count
        main = [
            jnp.concatenate([m[k * wide : (k + 1) * wide, :cut] for m in lhs], axis=0) for k in steps
        ]
        rest = [
            jnp.concatenate([m[k * wide : (k + 1) * wide, cut:] for m in lhs], axis=0) for k in steps
        ]
        hi, lo = split(jnp.concatenate(main + rest, axis=1))
        both = jnp.concatenate([hi, lo], axis=0)
        prod = jnp.dot(both, lhi[slot], preferred_element_type=F32)
        tail = jnp.dot(hi, llo[slot], preferred_element_type=F32)
        total = prod[: hi.shape[0]] + (prod[hi.shape[0] :] + tail)
        for lev in range(lev_count):
            re = total[lev * wide : lev * wide + SUB]
            im = total[lev * wide + SUB : (lev + 1) * wide]
            out[slot, lev * SUB : (lev + 1) * SUB] = jnp.stack([re, im], axis=1)
        store(slot).start()
        return carry

    lax.fori_loop(0, slot_count, body, 0)
    for slot in range(slot_count):
        store(slot).wait()


def legendre_step(waves, lhi, llo, grid_count, lev_count):
    slot_count, lat_total, total_count = lhi.shape
    chunks = waves.shape[0] // (grid_count * lev_count * slot_count)
    geo = (grid_count, lev_count, slot_count, chunks)
    out_shape = (slot_count, lev_count * SUB, 2, total_count)
    return pl.pallas_call(
        functools.partial(legendre_kernel, geo),
        out_shape=jax.ShapeDtypeStruct(out_shape, F32),
        in_specs=[pl.BlockSpec(memory_space=pltpu.VMEM)]
        + [pl.BlockSpec(memory_space=pltpu.HBM)] * 2,
        out_specs=pl.BlockSpec(memory_space=pltpu.HBM),
        scratch_shapes=[
            pltpu.VMEM(lhi.shape, BF16),
            pltpu.VMEM(llo.shape, BF16),
            pltpu.VMEM(out_shape, F32),
            pltpu.SemaphoreType.DMA(((2 * PIECES + 1) * slot_count,)),
        ],
        compiler_params=pltpu.CompilerParams(vmem_limit_bytes=50 * MIB),
        name="legendre_step",
    )(waves, lhi, llo)


def shards(trajectory, legendre, obs_cell, obs_count, departure, obs_weight, band_of, m_order):
    grid_count = lax.axis_size("grid")
    lev_count = lax.axis_size("lev")
    ch_dev, lat_dev, lon_count = trajectory.shape
    slot_count, lat_total, total_count = legendre.shape
    wave_total = m_order.shape[0]
    cells_per_dev = lat_dev * lon_count // LANES

    sent = pack(obs_count, departure, obs_weight, obs_cell, cells_per_dev)
    recv = lax.all_to_all(sent, "grid", split_axis=0, concat_axis=0, tiled=True)

    gain = jnp.swapaxes(1.0 + 0.5 * jnp.tanh(trajectory), 0, 1)
    thi, tlo = split_np(wave_table(wave_total, lon_count))
    cols = wave_columns(wave_total).reshape(1, -1)
    pick = (m_order[:, None] == cols).astype(BF16)

    waves = grid_to_waves(recv, gain, jnp.asarray(thi), jnp.asarray(tlo), pick)
    outgoing = waves.reshape(grid_count * lev_count, 1, -1)
    incoming = lax.all_to_all(
        outgoing, ("grid", "lev"), split_axis=0, concat_axis=0, tiled=True
    )

    lhi, llo = prepare_table(legendre, band_of, lat_dev)
    return legendre_step(
        incoming.reshape(-1, LANES), lhi, llo, grid_count, lev_count
    )


def solution(mesh):
    placed = (
        P("lev", "grid", None),
        P(("grid", "lev"), None, None),
        P("grid"),
        P("grid"),
        P("grid", None),
        P("lev", "grid"),
        P(),
        P(),
    )
    return jax.shard_map(
        shards,
        mesh=mesh,
        in_specs=placed,
        out_specs=P(("grid", "lev"), None, None, None),
        check_vma=False,
    )
```

```python
import functools
import math

import jax
import jax.numpy as jnp
import numpy as np
from jax import lax
from jax.experimental import pallas as pl
from jax.experimental.pallas import tpu as pltpu
from jax.sharding import PartitionSpec as P

LANES = 128
SUB = 8
RADIX = 16
GROUPS = RADIX // 2
MIB = 1 << 20
F32 = jnp.float32
BF16 = jnp.bfloat16
I32 = jnp.int32


def wave_columns(wave_total):
    per_residue = wave_total // RADIX
    cols = np.zeros((GROUPS, 2 * per_residue), np.int32)
    for g in range(GROUPS):
        first, second = g, (RADIX - g if g else RADIX // 2)
        turns = RADIX * np.arange(per_residue)
        cols[g, :per_residue] = first + turns
        cols[g, per_residue : 2 * per_residue] = second + turns
    return cols


def wave_table(wave_total, lon_count):
    width = lon_count // RADIX
    cols = wave_columns(wave_total)
    per_residue = wave_total // RADIX
    fine = np.arange(width, dtype=np.int64)
    out = np.zeros((GROUPS, 2, width, 2, LANES), np.float64)
    for g in range(GROUPS):
        for i in range(2 * per_residue):
            m = int(cols[g, i])
            lane = (g * 2 * per_residue + i) % LANES
            angle = 2.0 * math.pi / lon_count * ((m * fine) % lon_count)
            factor = 1.0 if m == 0 else 2.0
            cos, sin = factor * np.cos(angle), factor * np.sin(angle)
            second = i >= per_residue
            if g == 0:
                part = 1 if second else 0
                out[g, part, :, 0, lane] = cos
                out[g, part, :, 1, lane] = -sin
            else:
                sign = -1.0 if second else 1.0
                out[g, 0, :, 0, lane] = cos
                out[g, 1, :, 0, lane] = sign * sin
                out[g, 0, :, 1, lane] = -sin
                out[g, 1, :, 1, lane] = sign * cos
    return out.reshape(GROUPS, 2 * width, 2 * LANES).astype(np.float32)


def split_np(table):
    high = table.astype(jnp.bfloat16)
    low = (table - high.astype(np.float32)).astype(jnp.bfloat16)
    return high, low


def split(x):
    high = x.astype(BF16)
    return high, (x - high.astype(F32)).astype(BF16)


def real_fft(xs):
    n = len(xs)
    if n == 2:
        return [(xs[0] + xs[1], None), (xs[0] - xs[1], None)]
    even, odd = real_fft(xs[0::2]), real_fft(xs[1::2])
    out = [None] * (n // 2 + 1)
    for k in range(n // 4 + 1):
        er, ei = even[k]
        orr, oi = odd[k]
        if k == 0:
            out[0] = (er + orr, None)
            out[n // 2] = (er - orr, None)
        elif 4 * k == n:
            out[k] = (er, -orr)
        else:
            c, s = math.cos(2 * math.pi * k / n), math.sin(2 * math.pi * k / n)
            if 8 * k == n:
                tr, ti = (orr + oi) * c, (oi - orr) * c
            else:
                tr, ti = orr * c + oi * s, oi * c - orr * s
            out[k] = (er + tr, ei + ti)
            out[n // 2 - k] = (er - tr, ti - ei)
    return out


def pack_kernel(
    capacity, cells_per_dev, count_hbm, dep_hbm, weight_hbm, cell_hbm, out_hbm,
    counts, weights, cells_v, out, sems,
):
    groups = out.shape[0]
    small = [
        pltpu.make_async_copy(src, dst, sems.at[i])
        for i, (src, dst) in enumerate(
            ((count_hbm, counts), (weight_hbm, weights), (cell_hbm, cells_v))
        )
    ]
    for copy in small:
        copy.start()
    parts = 8
    each = groups // parts
    large = [
        pltpu.make_async_copy(
            dep_hbm.at[pl.ds(i * each, each)],
            out.at[pl.ds(i * each, each), pl.ds(0, capacity)],
            sems.at[3 + i],
        )
        for i in range(parts)
    ]
    for copy in large:
        copy.start()
    for copy in small:
        copy.wait()
    lane = lax.broadcasted_iota(I32, (SUB, LANES), 1)
    for q in range(groups):
        tile = q // 2
        weight = weights[:, tile * LANES : (tile + 1) * LANES]
        cells = jnp.broadcast_to(cells_v[tile : tile + 1, :], (SUB, LANES))
        cells = (cells - q * cells_per_dev).astype(F32)
        if q % 2:
            weight = pltpu.roll(weight, capacity, 1)
        else:
            cells = pltpu.roll(cells, capacity, 1)
        live = jnp.where(lane < counts[q], 1.0, 0.0)
        out[q, capacity:, :] = jnp.where(lane < capacity, weight * live, cells)
    sends = []
    for i in range(parts):
        large[i].wait()
        span = pl.ds(i * each, each)
        sends.append(
            pltpu.make_async_copy(out.at[span], out_hbm.at[span], sems.at[3 + parts + i])
        )
        sends[-1].start()
    for copy in sends:
        copy.wait()


def pack(obs_count, departure, obs_weight, obs_cell, cells_per_dev):
    groups = obs_count.shape[0]
    slots = departure.shape[0]
    capacity = slots // groups
    assert 2 * capacity == LANES and obs_weight.shape[0] == SUB
    cell_rows = obs_cell.reshape(slots // LANES, LANES)
    out_shape = (groups, capacity + SUB, LANES)
    return pl.pallas_call(
        functools.partial(pack_kernel, capacity, cells_per_dev),
        out_shape=jax.ShapeDtypeStruct(out_shape, F32),
        in_specs=[pl.BlockSpec(memory_space=pltpu.HBM)] * 4,
        out_specs=pl.BlockSpec(memory_space=pltpu.HBM),
        scratch_shapes=[
            pltpu.SMEM(obs_count.shape, I32),
            pltpu.VMEM(obs_weight.shape, F32),
            pltpu.VMEM(cell_rows.shape, I32),
            pltpu.VMEM(out_shape, F32),
            pltpu.SemaphoreType.DMA((19,)),
        ],
        compiler_params=pltpu.CompilerParams(vmem_limit_bytes=60 * MIB),
        name="pack",
    )(obs_count, departure.reshape(groups, capacity, LANES), obs_weight, cell_rows)


STREAMS = 1
AHEAD = 5


def grid_kernel(
    recv, gain_hbm, thi_hbm, tlo_hbm, pick_hbm, out_hbm, *scratch
):
    acc = scratch[:STREAMS]
    gain, thi, tlo, pick, cells_v, cells_s, lost_v, wide_a, wide_b, yhi, ylo, zt, out, sems = scratch[
        STREAMS:
    ]
    groups, rows_in, _ = recv.shape
    capacity = rows_in - SUB
    lat_dev = gain.shape[0]
    blocks = gain.shape[2] // LANES
    half = lat_dev // 2
    loads = [
        pltpu.make_async_copy(src, dst, sems.at[1 + i])
        for i, (src, dst) in enumerate(
            (
                (gain_hbm.at[pl.ds(0, half)], gain.at[pl.ds(0, half)]),
                (gain_hbm.at[pl.ds(half, half)], gain.at[pl.ds(half, half)]),
                (thi_hbm, thi),
                (tlo_hbm, tlo),
                (pick_hbm, pick),
            )
        )
    ]
    for copy in loads:
        copy.start()

    bunches = groups // SUB
    bunches = groups // SUB
    cells = recv[:, capacity, :].astype(I32)
    cells_v[...] = cells
    cell_copy = pltpu.make_async_copy(cells_v, cells_s, sems.at[0])
    cell_copy.start()

    inner = lax.broadcasted_iota(I32, (SUB, LANES), 0)
    lane = lax.broadcasted_iota(I32, (SUB, LANES), 1)
    for bunch in range(bunches):
        x = cells[bunch * SUB : (bunch + 1) * SUB]
        lost = jnp.full(x.shape, -1, I32)
        place = (bunch * SUB + inner) * LANES + lane
        for d in range(1, SUB):
            later = (x == pltpu.roll(x, SUB - d, 0)) & (inner < SUB - d) & (lane >= capacity)
            lost = jnp.where(later, place, lost)
        lost_v[bunch * SUB : (bunch + 1) * SUB] = lost.astype(F32)

    def clear(i, carry):
        for a in acc:
            a[pl.ds(i * SUB, SUB)] = jnp.zeros((SUB, SUB, LANES), F32)
        return carry

    lax.fori_loop(0, acc[0].shape[0] // SUB, clear, 0)


    rows = groups * SUB
    weight = recv[:, capacity:, :].reshape(rows, LANES)
    lane = lax.broadcasted_iota(I32, (rows, LANES), 1)
    whi, wlo = split(weight)
    both = jnp.where(
        lane < capacity, whi.astype(F32), pltpu.roll(wlo.astype(F32), capacity, 1)
    ).astype(BF16)
    row = lax.broadcasted_iota(I32, (LANES, 2 * LANES), 0) % capacity
    col = lax.broadcasted_iota(I32, (LANES, 2 * LANES), 1) // LANES
    offset = row - col

    def widen(ref, k0):
        ones = jnp.where(offset == k0, 1.0, 0.0).astype(BF16)
        ref[...] = jnp.dot(both, ones, preferred_element_type=F32)

    def add_slots(ref, k0, bunch):
        for kk in range(2):
            into = acc[(kk * bunches + bunch) % STREAMS]
            sources = range(bunch * SUB, (bunch + 1) * SUB)
            cells = [cells_s[s, capacity + k0 + kk] for s in sources]
            old = [into[c] for c in cells]
            new = []
            for o, s in zip(old, sources):
                weights = ref[s * SUB : (s + 1) * SUB, kk * LANES : (kk + 1) * LANES]
                new.append(o + weights * recv[s, pl.ds(k0 + kk, 1), :])
            for c, value in zip(cells, new):
                into[c] = value

    widen(wide_a, 0)
    cell_copy.wait()

    def scatter(i, carry):
        k0 = 4 * i
        widen(wide_b, k0 + 2)
        for bunch in range(bunches):
            add_slots(wide_a, k0, bunch)
        widen(wide_a, k0 + 4)
        for bunch in range(bunches):
            add_slots(wide_b, k0 + 2, bunch)
        return carry

    lax.fori_loop(0, capacity // 4, scatter, 0)

    def last_below(bound):
        x = lost_v[...]
        return jnp.max(jnp.where(x < bound, x, -1.0))

    def repair(code):
        place = code.astype(I32)
        s, k = place // LANES, place % LANES - capacity
        weights = recv[s, capacity:, :]
        column = lax.broadcasted_iota(I32, weights.shape, 1) == k
        weights = jnp.sum(jnp.where(column, weights, 0.0), axis=1, keepdims=True)
        acc[0][cells_s[s, capacity + k]] += weights * recv[s, pl.ds(k, 1), :]
        return last_below(code)

    lax.while_loop(lambda code: code >= 0.0, repair, last_below(float(groups * LANES)))

    for copy in loads[:2]:
        copy.wait()

    width = blocks // RADIX * LANES
    pair = 2

    def transform(i, carry):
        r0 = i * pair
        for h in range(blocks // RADIX):
            xs = []
            for a in range(RADIX):
                b = a * (blocks // RADIX) + h
                parts = []
                for r in range(pair):
                    cell = (r0 + r) * blocks + b
                    total = acc[0][cell]
                    for t in range(1, STREAMS):
                        total = total + acc[t][cell]
                    parts.append(total * gain[r0 + r, :, b * LANES : (b + 1) * LANES])
                xs.append(jnp.concatenate(parts, axis=0))
            ys = real_fft(xs)
            rows = pl.ds(pl.multiple_of(r0 * SUB, pair * SUB), pair * SUB)
            for g in range(GROUPS):
                re, im = ys[g] if g else (ys[0][0], ys[RADIX // 2][0])
                for part, value in enumerate((re, im)):
                    lanes = pl.ds(part * width + h * LANES, LANES)
                    hi, lo = split(value)
                    yhi[g, rows, lanes] = hi
                    ylo[g, rows, lanes] = lo
        return carry

    lax.fori_loop(0, lat_dev // pair, transform, 0)
    for copy in loads[2:]:
        copy.wait()

    def dot(a, b):
        return jnp.dot(a, b, preferred_element_type=F32)

    waves = pick.shape[0]
    members = waves // GROUPS
    lane = lax.broadcasted_iota(I32, (2 * lat_dev * SUB, LANES), 1)
    open_tile = None
    for g in range(GROUPS):
        high, top = yhi[g], thi[g]
        z = dot(
            jnp.concatenate([high, high, ylo[g]], axis=1),
            jnp.concatenate([top, tlo[g], top], axis=0),
        )
        re = z[:, :LANES].reshape(lat_dev, 1, SUB, LANES)
        im = z[:, LANES:].reshape(lat_dev, 1, SUB, LANES)
        both = jnp.concatenate([re, im], axis=1).reshape(lat_dev * 2 * SUB, LANES)
        tile, offset = divmod(g * members, LANES)
        past = offset + members - LANES
        mine = jnp.where(lane >= offset, both, 0.0) if past > 0 else both
        open_tile = mine if open_tile is None else open_tile + mine
        if past >= 0:
            hi, lo = split(open_tile.T)
            zt[tile * LANES : (tile + 1) * LANES, :] = hi
            zt[waves + tile * LANES : waves + (tile + 1) * LANES, :] = lo
            open_tile = jnp.where(lane < past, both, 0.0) if past > 0 else None

    chunks = zt.shape[1] // LANES
    tall = LANES
    sends = []
    for j0 in range(0, waves, tall):
        sel = pick[j0 : j0 + tall, :]
        res = dot(jnp.concatenate([sel, sel], axis=1), zt[...])
        for jt in range(tall // SUB):
            for c in range(chunks):
                start = (j0 + jt * SUB) * chunks + c
                out[pl.ds(start, SUB, stride=chunks), :] = res[
                    jt * SUB : (jt + 1) * SUB, c * LANES : (c + 1) * LANES
                ]
        span = pl.ds(j0 * chunks, tall * chunks)
        sends.append(
            pltpu.make_async_copy(out.at[span], out_hbm.at[span], sems.at[6 + j0 // tall])
        )
        sends[-1].start()
    for copy in sends:
        copy.wait()


def grid_to_waves(recv, gain, thi, tlo, pick):
    lat_dev, ch_dev, lon_count = gain.shape
    waves = pick.shape[0]
    groups, capacity = recv.shape[0], recv.shape[1] - SUB
    cells = lat_dev * lon_count // LANES
    rows = lat_dev * ch_dev
    return pl.pallas_call(
        grid_kernel,
        out_shape=jax.ShapeDtypeStruct((waves * 2 * rows // LANES, LANES), F32),
        in_specs=[pl.BlockSpec(memory_space=pltpu.VMEM)]
        + [pl.BlockSpec(memory_space=pltpu.HBM)] * 4,
        out_specs=pl.BlockSpec(memory_space=pltpu.HBM),
        scratch_shapes=[pltpu.VMEM((cells, ch_dev, LANES), F32) for _ in range(STREAMS)]
        + [
            pltpu.VMEM(gain.shape, F32),
            pltpu.VMEM(thi.shape, BF16),
            pltpu.VMEM(tlo.shape, BF16),
            pltpu.VMEM(pick.shape, BF16),
            pltpu.VMEM((groups, LANES), I32),
            pltpu.SMEM((groups, LANES), I32),
            pltpu.VMEM((groups, LANES), F32),
            pltpu.VMEM((groups * SUB, 2 * LANES), F32),
            pltpu.VMEM((groups * SUB, 2 * LANES), F32),
            pltpu.VMEM((GROUPS, rows, thi.shape[1]), BF16),
            pltpu.VMEM((GROUPS, rows, thi.shape[1]), BF16),
            pltpu.VMEM((2 * waves, 2 * rows), BF16),
            pltpu.VMEM((waves * 2 * rows // LANES, LANES), F32),
            pltpu.SemaphoreType.DMA((6 + waves // LANES,)),
        ],
        compiler_params=pltpu.CompilerParams(vmem_limit_bytes=52 * MIB),
        name="grid_to_waves",
    )(recv, gain, thi, tlo, pick)


def prepare_kernel(lat_dev, band_ref, table_ref, hi_ref, lo_ref):
    grid_count = band_ref.shape[0]
    chunks = lat_dev // SUB
    full = LANES // grid_count
    assert chunks == full + 1
    half = 2 * SUB

    def body(c, carry):
        starts = [
            pl.multiple_of(band_ref[g] * lat_dev + c * SUB, SUB) for g in range(grid_count)
        ]
        for t in range(table_ref.shape[2] // LANES):
            lanes = pl.ds(t * LANES, LANES)
            for g0 in range(0, grid_count, half):
                turned = []
                for g1 in range(g0, g0 + half, SUB):
                    tiles = [
                        table_ref[0, pl.ds(starts[g], SUB), lanes] for g in range(g1, g1 + SUB)
                    ]
                    turned.append(jnp.swapaxes(jnp.stack(tiles), 0, 1))
                for k in range(SUB):
                    hi, lo = split(jnp.concatenate([x[k] for x in turned], axis=0))
                    start = jnp.where(
                        c < full, k * LANES + c * grid_count, full * SUB * grid_count + k * grid_count
                    )
                    start = pl.multiple_of(start + g0, half)
                    hi_ref[0, pl.ds(start, half), lanes] = hi
                    lo_ref[0, pl.ds(start, half), lanes] = lo
        return carry

    lax.fori_loop(0, chunks, body, 0)


def prepare_table(legendre, band_of, lat_dev):
    slot_count, lat_total, total_count = legendre.shape
    block = pl.BlockSpec((1, lat_total, total_count), lambda s: (s, 0, 0))
    return pl.pallas_call(
        functools.partial(prepare_kernel, lat_dev),
        grid=(slot_count,),
        out_shape=[jax.ShapeDtypeStruct(legendre.shape, BF16)] * 2,
        in_specs=[pl.BlockSpec(memory_space=pltpu.SMEM), block],
        out_specs=[block, block],
        compiler_params=pltpu.CompilerParams(vmem_limit_bytes=56 * MIB),
        cost_estimate=pl.CostEstimate(
            flops=4 * legendre.size, bytes_accessed=8 * legendre.size, transcendentals=0
        ),
        name="prepare_table",
    )(band_of, legendre)


def legendre_kernel(geo, x_ref, lhi_hbm, llo_hbm, out_hbm, lhi, llo, out, sems):
    grid_count, lev_count, slot_count, chunks = geo
    full = LANES // grid_count
    wide = 2 * SUB
    def loads(slot):
        return [
            pltpu.make_async_copy(src.at[slot], dst.at[slot], sems.at[2 * slot + i])
            for i, (src, dst) in enumerate(((lhi_hbm, lhi), (llo_hbm, llo)))
        ]

    for slot in range(AHEAD):
        for copy in loads(slot):
            copy.start()

    def store(slot):
        return pltpu.make_async_copy(
            out.at[slot], out_hbm.at[slot], sems.at[2 * slot_count + slot]
        )

    def body(slot, carry):
        lhs = []
        for lev in range(lev_count):
            pieces = []
            for c in range(chunks):
                start = (lev * slot_count + slot) * chunks + c
                pieces.append(
                    x_ref[pl.ds(start, grid_count, stride=lev_count * slot_count * chunks), :]
                )
            lhs.append(jnp.concatenate(pieces, axis=0).T)
        for copy in loads(slot):
            copy.wait()

        @pl.when(slot + AHEAD < slot_count)
        def _():
            for copy in loads(slot + AHEAD):
                copy.start()

        steps = range(LANES // wide)
        cut = full * grid_count
        main = [
            jnp.concatenate([m[k * wide : (k + 1) * wide, :cut] for m in lhs], axis=0) for k in steps
        ]
        rest = [
            jnp.concatenate([m[k * wide : (k + 1) * wide, cut:] for m in lhs], axis=0) for k in steps
        ]
        hi, lo = split(jnp.concatenate(main + rest, axis=1))
        both = jnp.concatenate([hi, lo], axis=0)
        prod = jnp.dot(both, lhi[slot], preferred_element_type=F32)
        tail = jnp.dot(hi, llo[slot], preferred_element_type=F32)
        total = prod[: hi.shape[0]] + (prod[hi.shape[0] :] + tail)
        for lev in range(lev_count):
            re = total[lev * wide : lev * wide + SUB]
            im = total[lev * wide + SUB : (lev + 1) * wide]
            out[slot, lev * SUB : (lev + 1) * SUB] = jnp.stack([re, im], axis=1)
        store(slot).start()
        return carry

    lax.fori_loop(0, slot_count, body, 0)
    for slot in range(slot_count):
        store(slot).wait()


def legendre_step(waves, lhi, llo, grid_count, lev_count):
    slot_count, lat_total, total_count = lhi.shape
    chunks = waves.shape[0] // (grid_count * lev_count * slot_count)
    geo = (grid_count, lev_count, slot_count, chunks)
    out_shape = (slot_count, lev_count * SUB, 2, total_count)
    return pl.pallas_call(
        functools.partial(legendre_kernel, geo),
        out_shape=jax.ShapeDtypeStruct(out_shape, F32),
        in_specs=[pl.BlockSpec(memory_space=pltpu.VMEM)]
        + [pl.BlockSpec(memory_space=pltpu.HBM)] * 2,
        out_specs=pl.BlockSpec(memory_space=pltpu.HBM),
        scratch_shapes=[
            pltpu.VMEM(lhi.shape, BF16),
            pltpu.VMEM(llo.shape, BF16),
            pltpu.VMEM(out_shape, F32),
            pltpu.SemaphoreType.DMA((3 * slot_count,)),
        ],
        compiler_params=pltpu.CompilerParams(vmem_limit_bytes=50 * MIB),
        name="legendre_step",
    )(waves, lhi, llo)


def shards(trajectory, legendre, obs_cell, obs_count, departure, obs_weight, band_of, m_order):
    grid_count = lax.axis_size("grid")
    lev_count = lax.axis_size("lev")
    ch_dev, lat_dev, lon_count = trajectory.shape
    slot_count, lat_total, total_count = legendre.shape
    wave_total = m_order.shape[0]
    cells_per_dev = lat_dev * lon_count // LANES

    sent = pack(obs_count, departure, obs_weight, obs_cell, cells_per_dev)
    recv = lax.all_to_all(sent, "grid", split_axis=0, concat_axis=0, tiled=True)

    gain = jnp.swapaxes(1.0 + 0.5 * jnp.tanh(trajectory), 0, 1)
    thi, tlo = split_np(wave_table(wave_total, lon_count))
    cols = wave_columns(wave_total).reshape(1, -1)
    pick = (m_order[:, None] == cols).astype(BF16)

    waves = grid_to_waves(recv, gain, jnp.asarray(thi), jnp.asarray(tlo), pick)
    outgoing = waves.reshape(grid_count * lev_count, 1, -1)
    incoming = lax.all_to_all(
        outgoing, ("grid", "lev"), split_axis=0, concat_axis=0, tiled=True
    )

    lhi, llo = prepare_table(legendre, band_of, lat_dev)
    return legendre_step(
        incoming.reshape(-1, LANES), lhi, llo, grid_count, lev_count
    )


def solution(mesh):
    placed = (
        P("lev", "grid", None),
        P(("grid", "lev"), None, None),
        P("grid"),
        P("grid"),
        P("grid", None),
        P("lev", "grid"),
        P(),
        P(),
    )
    return jax.shard_map(
        shards,
        mesh=mesh,
        in_specs=placed,
        out_specs=P(("grid", "lev"), None, None, None),
        check_vma=False,
    )
```
